256 devices in a mesh: blk: 64 (over y, z, core), span: 4 (over x).
Axes of the slice: x: 4, y: 4, z: 8, core: 2. Of those that a mesh axis runs over, the one named last changes fastest.
Arguments:
- velocity: float32 [3, 1024, 128, 128], P(None, 'blk', 'span'), may hold values from -6 to 6
- stretch: float32 [3, 1024, 128, 128], P(None, 'blk', 'span'), may hold values from 0.5 to 2
- coupling: float32 [1024, 128, 128], P('blk', 'span'), may hold values from 0.05 to 0.5
- strengths: bfloat16 [32768, 128], P(('blk', 'span')), may hold values from -6 to 6
- remesh: bfloat16 [2097152, 128], P(('blk', 'span')), may hold values from -0.5 to 0.5
- green_left: bfloat16 [128, 128], replicated, may hold values from -0.5 to 0.5
- green_right: bfloat16 [128, 128], replicated, may hold values from -0.5 to 0.5
- tile_owner: int32 [16384, 1], replicated, may hold values from 0 to 63; in each aligned block of 64 rows (0 to 63, 64 to 127, ...) at most 2 rows name the same one
- tile_place: int32 [16384], replicated, may hold values from 0 to 11
- row_dest: int32 [393216, 1], replicated, may hold values from 0 to 63; in each aligned block of 1536 rows (0 to 1535, 1536 to 3071, ...) at most 48 rows name the same one
- row_place: int32 [393216], replicated, may hold values from 0 to 8191
Outputs:
- velocity_next: float32 [3, 1024, 128, 128], P(None, 'blk', 'span')
- strengths_next: float32 [32768, 128], P(('blk', 'span'))
The draws below stay inside these ranges and needn't reach their ends.
Inputs may be any that keep to these rules, and one draw needn't show every extreme that they name: `tile_owner`: among the 64 tiles of one box, no chord block is named by more than 2, and one is named by exactly 2. `row_dest`: among the 1536 rows of one grid block, no chord block is named by more than 48, and one is named by exactly 48.
All inputs are finite; a program needn't handle non-finite values.
Results may differ from the reference program's by a relative error of at most 0.004.
Values may be sent and summed in bfloat16 or wider, within the bound.
No kernel may reach another device: no remote copies, remote signals or barrier semaphores. Data moves between devices by JAX's collectives and lax.ppermute only.
A program may use at most 128 MiB of HBM per device.

```python
import math
import jax
import jax.numpy as jnp
import numpy as np
from jax import lax

EDGE = 128
CX = 16
CS = 32
TILES_DEV = 64
PART_ROWS = 128
SWEEPS = 2
NX = 1024
NS = 128
GRID_ROWS = 1536
FACE = 12
BOX_ROWS = 8192
CAP_T = 2
CAP_R = 48
N_BLK = 64
N_SPAN = 4


def set_ends(drawn, key, least, largest):
    longest = drawn.shape.index(max(drawn.shape))
    spots = []
    for shift in (0, 1):
        where = [jax.random.randint(jax.random.fold_in(key, axis), (), 0, length) for axis, length in enumerate(drawn.shape)]
        where[longest] = (where[longest] + shift) % drawn.shape[longest]
        spots.append(tuple(where))
    return drawn.at[spots[0]].set(least).at[spots[1]].set(largest)


def levels(key, dims, pieces, smallest, top_value):
    factor_of, own = 1.0, jax.random.fold_in(key, 6)
    for axis_at, parts in pieces:
        steps = jnp.exp(jax.random.uniform(jax.random.fold_in(own, axis_at), (parts,), jnp.float32, smallest / len(pieces), top_value / len(pieces)))
        factor_of = factor_of * jnp.repeat(steps, dims[axis_at] // parts).reshape([-1 if axis == axis_at else 1 for axis in range(len(dims))])
    return factor_of


def shared_out(own_key, own, number, rows, number_of, top, most, skew):
    ranking = jax.random.permutation(own_key, number_of)
    heavy_load, common = load_shares(number_of, rows * top, most, skew, True), load_shares(number_of, rows * top, most, skew, False)
    places = jnp.arange(number_of)

    def named(sizes, turn):
        used = int((sizes > 0).sum())
        fixed = max(1, used // 4)
        shifted = fixed + (places - fixed + turn * (used - fixed)) % max(1, number_of - fixed)
        return jnp.zeros((number_of,), jnp.int32).at[ranking[jnp.where(places < fixed, places, shifted)]].set(jnp.asarray(sizes, jnp.int32))

    sizes = jnp.where(number % 4 == 0, named(heavy_load, number // 4), named(common, number - number // 4 - 1))
    mixed = jax.random.permutation(jax.random.fold_in(own, 3), number_of)
    donor, receiver = mixed[0:number_of // 2 * 2:2], mixed[1:number_of // 2 * 2:2]
    margin = jnp.minimum(sizes[donor] - 1, most - sizes[receiver]) // 2
    margin = jnp.where((donor == ranking[0]) | (receiver == ranking[0]) | (sizes[receiver] == 0), 0, jnp.maximum(margin, 0))
    shifted = jax.random.randint(jax.random.fold_in(own, 4), (number_of // 2,), 0, 1 << 20) % (margin + 1)
    sizes = sizes.at[donor].add(-shifted).at[receiver].add(shifted)
    labels = jnp.searchsorted(jnp.cumsum(sizes), jnp.arange(rows * top), side="right").astype(jnp.int32)
    table = labels.reshape(top, rows).T
    table = table[jax.random.permutation(jax.random.fold_in(own, 1), rows)]
    turn = jax.random.randint(jax.random.fold_in(own, 2), (rows, 1), 0, top)
    return jnp.take_along_axis(table, (jnp.arange(top)[None, :] + turn) % top, axis=1)


def load_shares(count, total, most, slope, full):
    loads = [(1 << 20) // math.isqrt(standing ** slope) + 1 for standing in range(1, count + 1)]
    largest = most if full else min(most, max(-(-total // count), total * loads[0] // sum(loads)))
    least = 1 if total - largest >= count - 1 else 0
    given, surplus = [largest] + [least] * (count - 1), total - largest - least * (count - 1)
    while surplus > 0:
        candidates = [i for i in range(1, count) if given[i] < largest] or [i for i in range(1, count) if given[i] < most]
        pool, remaining = sum([loads[i] for i in candidates]), surplus
        for i in candidates:
            addition = min(most - given[i], max(1, remaining * loads[i] // pool), surplus)
            given[i] = given[i] + addition
            surplus = surplus - addition
    return np.array(given)


def noise(own_key, dims, scale, bound, cuts=(), held_as=jnp.bfloat16):
    values = jax.random.normal(own_key, dims, jnp.float32) * scale
    if len(cuts) > 0:
        values = levels(own_key, dims, cuts, -0.22, 0.18) * values
    return jnp.clip(values, min=-bound, max=bound).astype(held_as)


def setup_inputs(seed: int = 0) -> dict:
    streams_of = jax.random.split(jax.random.key(seed), 12)
    velocity = noise(streams_of[0], (3, NX, NS, EDGE), 1.0, 6.0, ((1, 64), (2, 4)), jnp.float32)
    stretch = jnp.clip(jnp.exp(math.log(2.0) - 1.3862944 * jax.random.uniform(streams_of[1], (3, NX, NS, EDGE), jnp.float32) ** levels(streams_of[1], (3, NX, NS, EDGE), ((1, 64), (2, 4)), -0.2, 0.2)), 0.5, 2.0)
    coupling = jnp.clip(jnp.exp(math.log(0.5) - 2.3025851 * jax.random.uniform(streams_of[2], (NX, NS, EDGE), jnp.float32) ** levels(streams_of[2], (NX, NS, EDGE), ((0, 64), (1, 4)), -0.2, 0.2)), 0.05, 0.5)
    strengths = noise(streams_of[3], (N_BLK * N_SPAN * PART_ROWS, EDGE), 1.0, 6.0, ((0, 256),))
    remesh = noise(streams_of[4], (N_BLK * N_SPAN * BOX_ROWS, PART_ROWS), PART_ROWS ** -0.5, 0.5, ((0, 256),))
    green_left = noise(streams_of[5], (EDGE, EDGE), EDGE ** -0.5, 0.5)
    green_right = noise(streams_of[6], (EDGE, EDGE), EDGE ** -0.5, 0.5)
    tile_owner_keys = jax.random.split(jax.random.fold_in(streams_of[7], 1), (N_BLK * N_SPAN * TILES_DEV) // TILES_DEV)
    tile_owner_turns = jax.random.permutation(jax.random.fold_in(streams_of[7], 3), (N_BLK * N_SPAN * TILES_DEV) // TILES_DEV)
    tile_owner = jax.vmap(lambda own, number: shared_out(jax.random.fold_in(streams_of[7], 2), own, number, TILES_DEV, N_BLK, 1, CAP_T, 2))(tile_owner_keys, tile_owner_turns).reshape((N_BLK * N_SPAN * TILES_DEV, 1))
    tile_place = set_ends(jax.random.randint(streams_of[8], (N_BLK * N_SPAN * TILES_DEV,), 0, FACE), jax.random.fold_in(streams_of[8], 1), 0, FACE - 1).astype(jnp.int32)
    row_dest_keys = jax.random.split(jax.random.fold_in(streams_of[9], 1), (N_BLK * N_SPAN * GRID_ROWS) // GRID_ROWS)
    row_dest_turns = jax.random.permutation(jax.random.fold_in(streams_of[9], 3), (N_BLK * N_SPAN * GRID_ROWS) // GRID_ROWS)
    row_dest = jax.vmap(lambda own, number: shared_out(jax.random.fold_in(streams_of[9], 2), own, number, GRID_ROWS, N_BLK, 1, CAP_R, 1))(row_dest_keys, row_dest_turns).reshape((N_BLK * N_SPAN * GRID_ROWS, 1))
    row_place = set_ends(jax.random.randint(streams_of[10], (N_BLK * N_SPAN * GRID_ROWS,), 0, BOX_ROWS), jax.random.fold_in(streams_of[10], 1), 0, BOX_ROWS - 1).astype(jnp.int32)
    return dict(velocity=velocity, stretch=stretch, coupling=coupling, strengths=strengths, remesh=remesh, green_left=green_left, green_right=green_right, tile_owner=tile_owner, tile_place=tile_place, row_dest=row_dest, row_place=row_place)


step_size = 0.05
viscosity = 0.4
blend = 0.5


def neighbours(padded):
    centre = padded[:, 1:-1, 1:-1, :]
    normal_pad = jnp.pad(centre, ((0, 0), (0, 0), (0, 0), (1, 1)))
    forward = (padded[:, 2:, 1:-1, :], padded[:, 1:-1, 2:, :], normal_pad[:, :, :, 2:])
    backward = (padded[:, :-2, 1:-1, :], padded[:, 1:-1, :-2, :], normal_pad[:, :, :, :-2])
    return centre, forward, backward


def advance(padded, stretch, coupling, target):
    centre, forward, backward = neighbours(padded)
    laplace = jnp.zeros_like(centre)
    advection = jnp.zeros_like(centre)
    for direction in range(3):
        metric = stretch[direction]
        laplace = laplace + metric * metric * (forward[direction] + backward[direction] - 2.0 * centre)
        advection = advection + 0.5 * metric * centre[direction] * (forward[direction] - backward[direction])
    return centre + step_size * (viscosity * laplace - advection) + coupling * (target - centre)


def rotation(padded, stretch):
    centre, forward, backward = neighbours(padded)

    def derivative(direction, component):
        return 0.5 * stretch[direction] * (forward[direction][component] - backward[direction][component])

    along_chord = derivative(1, 2) - derivative(2, 1)
    along_span = derivative(2, 0) - derivative(0, 2)
    along_normal = derivative(0, 1) - derivative(1, 0)
    return jnp.stack([along_chord, along_span, along_normal])


def with_rim(values):
    return jnp.pad(values, ((0, 0), (1, 1), (1, 1), (0, 0)))


def reference(velocity, stretch, coupling, strengths, remesh, green_left, green_right, tile_owner, tile_place, row_dest, row_place):
    device_count = N_BLK * N_SPAN
    owners = tile_owner.reshape(device_count, TILES_DEV)
    places = tile_place.reshape(device_count, TILES_DEV)
    strength_boxes = strengths.reshape(device_count, PART_ROWS, EDGE)
    remesh_boxes = remesh.reshape(device_count, BOX_ROWS, PART_ROWS)
    left_green = green_left.astype(jnp.float32)
    right_green = green_right.astype(jnp.float32)
    highest = lax.Precision.HIGHEST

    def gather_tiles(totals, item):
        device, weights, sources, owner_list, place_list = item
        vortex_box = jnp.dot(weights, sources, preferred_element_type=jnp.float32).astype(jnp.bfloat16)
        vortex_tiles = vortex_box.astype(jnp.float32).reshape(TILES_DEV, EDGE, EDGE)
        half_product = jnp.einsum("ab,tbk->tak", left_green, vortex_tiles, precision=highest)
        induced = jnp.einsum("tak,kl->tal", half_product, right_green, precision=highest)
        totals = totals.at[owner_list, device % N_SPAN, place_list].add(induced.reshape(TILES_DEV, EDGE * EDGE))
        return totals, None

    totals = jnp.zeros((N_BLK, N_SPAN, FACE, EDGE * EDGE), jnp.float32)
    device_ids = jnp.arange(device_count, dtype=jnp.int32)
    totals, unused = lax.scan(gather_tiles, totals, (device_ids, remesh_boxes, strength_boxes, owners, places))
    target = totals.reshape(N_BLK, N_SPAN, 3, CX, CS, EDGE).transpose(2, 0, 3, 1, 4, 5).reshape(3, N_BLK * CX, N_SPAN * CS, EDGE)

    current = velocity
    for sweep_index in range(SWEEPS):
        current = advance(with_rim(current), stretch, coupling, target)
    vorticity = rotation(with_rim(current), stretch).astype(jnp.bfloat16)
    grid_rows = vorticity.reshape(3, N_BLK, CX, N_SPAN, CS, EDGE).transpose(1, 3, 0, 2, 4, 5).reshape(N_BLK, N_SPAN, GRID_ROWS, EDGE)
    destinations = row_dest.reshape(N_BLK, N_SPAN, GRID_ROWS)
    row_places = row_place.reshape(N_BLK, N_SPAN, GRID_ROWS)

    def update_box(item):
        device, weights, sources = item
        chord_block = device // N_SPAN
        span_piece = device % N_SPAN
        column_rows = lax.dynamic_index_in_dim(grid_rows, span_piece, 1, keepdims=False).reshape(N_BLK * GRID_ROWS, EDGE)
        column_dest = lax.dynamic_index_in_dim(destinations, span_piece, 1, keepdims=False).reshape(N_BLK * GRID_ROWS)
        column_place = lax.dynamic_index_in_dim(row_places, span_piece, 1, keepdims=False).reshape(N_BLK * GRID_ROWS)
        kept = (column_dest == chord_block).astype(jnp.float32)
        placed = jax.ops.segment_sum(column_rows.astype(jnp.float32) * kept[:, None], column_place, num_segments=BOX_ROWS)
        spread = lax.dot_general(weights, placed.astype(jnp.bfloat16), (((0,), (0,)), ((), ())), preferred_element_type=jnp.float32)
        return (1.0 - blend) * sources.astype(jnp.float32) + blend * spread

    updated = lax.map(update_box, (device_ids, remesh_boxes, strength_boxes))
    return current, updated.reshape(device_count * PART_ROWS, EDGE)
```

```python
import jax
import jax.numpy as jnp
from jax import lax
from jax.experimental import pallas as pl
from jax.experimental.pallas import tpu as pltpu
from jax.sharding import PartitionSpec as P

step_size = 0.05
viscosity = 0.4
blend = 0.5

EDGE = 128
REACH = 3
SIDE = 8
GROUP = 16


def pieces_kernel(remesh_ref, strengths_ref, left_ref, out_ref, scratch):
    vortex = jnp.dot(
        remesh_ref[...], strengths_ref[...], preferred_element_type=jnp.float32
    ).astype(jnp.bfloat16)
    left = left_ref[...]
    for pair in range(GROUP // 2):
        first = vortex[(2 * pair) * EDGE : (2 * pair + 1) * EDGE]
        second = vortex[(2 * pair + 1) * EDGE : (2 * pair + 2) * EDGE]
        both = jnp.dot(
            left, jnp.concatenate([first, second], axis=1), preferred_element_type=jnp.float32
        )
        for half in range(2):
            tile = 2 * pair + half
            for quarter in range(4):
                for side in range(2):
                    start = quarter * 32 + side * 16
                    scratch[
                        side, pl.ds(quarter * 16 * GROUP + tile, 16, stride=GROUP), :
                    ] = both[start : start + 16, half * EDGE : (half + 1) * EDGE]
    for side in range(2):
        out_ref[:, :, side * EDGE : (side + 1) * EDGE] = (
            scratch[side].astype(jnp.bfloat16).reshape(64, GROUP, EDGE)
        )


def tile_pieces(remesh, strengths, left):
    tiles = remesh.shape[0] // EDGE
    return pl.pallas_call(
        pieces_kernel,
        grid=(tiles // GROUP,),
        in_specs=[
            pl.BlockSpec((GROUP * EDGE, EDGE), lambda g: (g, 0)),
            pl.BlockSpec((EDGE, EDGE), lambda g: (0, 0)),
            pl.BlockSpec((EDGE, EDGE), lambda g: (0, 0)),
        ],
        out_specs=pl.BlockSpec((64, GROUP, 2 * EDGE), lambda g: (0, g, 0)),
        out_shape=jax.ShapeDtypeStruct((64, tiles, 2 * EDGE), jnp.bfloat16),
        scratch_shapes=[pltpu.VMEM((2, 64 * GROUP, EDGE), jnp.float32)],
        compiler_params=pltpu.CompilerParams(vmem_limit_bytes=32 * 1024 * 1024),
    )(remesh, strengths, left)


def gather_kernel(index_ref, remesh_ref, out_ref, wide, picked):
    wide[...] = remesh_ref[...].astype(jnp.float32)

    def some(step, carry):
        for k in range(16):
            slot = step * 16 + k
            picked[pl.ds(slot, 1), :] = wide[pl.ds(index_ref[slot], 1), :]
        return carry

    lax.fori_loop(0, out_ref.shape[0] // 16, some, 0)
    out_ref[...] = picked[...].astype(jnp.bfloat16)


def gathered_rows(index, remesh):
    slots = index.shape[0]
    return pl.pallas_call(
        gather_kernel,
        in_specs=[
            pl.BlockSpec(memory_space=pltpu.SMEM),
            pl.BlockSpec(memory_space=pltpu.VMEM),
        ],
        out_specs=pl.BlockSpec(memory_space=pltpu.VMEM),
        out_shape=jax.ShapeDtypeStruct((slots, EDGE), jnp.bfloat16),
        scratch_shapes=[
            pltpu.VMEM(remesh.shape, jnp.float32),
            pltpu.VMEM((slots, EDGE), jnp.float32),
        ],
        compiler_params=pltpu.CompilerParams(vmem_limit_bytes=40 * 1024 * 1024),
        cost_estimate=pl.CostEstimate(flops=0, bytes_accessed=16 * 1024 * 1024, transcendentals=0),
    )(index, remesh)


def grid_kernel(
    sums_ref,
    low_ref,
    high_ref,
    right_ref,
    fields_ref,
    next_ref,
    rows_ref,
    centre_sums,
    side_sums,
    target,
    first,
    second,
):
    right = right_ref[...]
    span = 32
    wide = span + 2 * SIDE
    for side in range(2):
        centre_sums[side] = jnp.dot(
            sums_ref[:, side * EDGE : (side + 1) * EDGE], right, preferred_element_type=jnp.float32
        )
    side_sums[0] = jnp.dot(low_ref[...], right, preferred_element_type=jnp.float32)
    side_sums[1] = jnp.dot(high_ref[...], right, preferred_element_type=jnp.float32)
    for component in range(3):
        for layer in range(20):
            chord = layer - 2
            quarter = chord % 4
            entry = component * 4 + chord // 4 if 0 <= chord < 16 else 12 + component
            for side in range(2):
                target[component, layer, SIDE + 16 * side : SIDE + 16 * side + 16, :] = centre_sums[
                    side, pl.ds(quarter * 256 + entry, 16, stride=16), :
                ]
            target[component, layer, SIDE - 2 : SIDE, :] = side_sums[
                0, pl.ds(quarter * 32 + entry, 2, stride=16), :
            ]
            target[component, layer, SIDE + span : SIDE + span + 2, :] = side_sums[
                1, pl.ds(quarter * 32 + entry, 2, stride=16), :
            ]

    lanes = lax.broadcasted_iota(jnp.int32, (wide, EDGE), 1)
    not_last = lanes < EDGE - 1
    not_first = lanes > 0

    def after(value, direction):
        if direction == 1:
            return pltpu.roll(value, wide - 1, 0)
        return jnp.where(not_last, pltpu.roll(value, EDGE - 1, 1), 0.0)

    def before(value, direction):
        if direction == 1:
            return pltpu.roll(value, 1, 0)
        return jnp.where(not_first, pltpu.roll(value, 1, 1), 0.0)

    def advanced(source, at, layer, target_layer):
        centre = [source[c, at] for c in range(3)]
        stretch = [fields_ref[3 + d, layer] for d in range(3)]
        rate = fields_ref[6, layer]
        squares = [(step_size * viscosity) * s * s for s in stretch]
        carried = [(0.5 * step_size) * s * u for s, u in zip(stretch, centre)]
        results = []
        for c in range(3):
            value = centre[c]
            twice = 2.0 * value
            change = rate * (target[c, target_layer] - value)
            for d in range(3):
                if d == 0:
                    ahead, behind = source[c, at + 1], source[c, at - 1]
                else:
                    ahead, behind = after(value, d), before(value, d)
                change = change + squares[d] * (ahead + behind - twice)
                change = change - carried[d] * (ahead - behind)
            results.append(value + change)
        return results

    def first_step(layer, carry):
        results = advanced(fields_ref, layer + 1, layer + 1, layer)
        for c in range(3):
            first[c, layer] = results[c]
        return carry

    lax.fori_loop(0, 20, first_step, 0)

    def second_step(layer, carry):
        results = advanced(first, layer + 1, layer + 2, layer + 1)
        for c in range(3):
            second[c, layer] = results[c]
        return carry

    lax.fori_loop(0, 18, second_step, 0)

    def curl(layer, carry):
        centre = [second[c, layer + 1] for c in range(3)]
        half = [0.5 * fields_ref[3 + d, layer + 3] for d in range(3)]

        def slope(d, c):
            if d == 0:
                return half[0] * (second[c, layer + 2] - second[c, layer])
            return half[d] * (after(centre[c], d) - before(centre[c], d))

        parts = (
            slope(1, 2) - slope(2, 1),
            slope(2, 0) - slope(0, 2),
            slope(0, 1) - slope(1, 0),
        )
        for c in range(3):
            rows_ref[c, layer] = parts[c][SIDE : SIDE + span].astype(jnp.bfloat16)
            next_ref[c, layer] = centre[c][SIDE : SIDE + span]
        return carry

    lax.fori_loop(0, 16, curl, 0)


def grid_update(sums, low, high, right, fields):
    wide = 32 + 2 * SIDE
    vmem = pl.BlockSpec(memory_space=pltpu.VMEM)
    return pl.pallas_call(
        grid_kernel,
        in_specs=[vmem] * 5,
        out_specs=[vmem] * 2,
        out_shape=[
            jax.ShapeDtypeStruct((3, 16, 32, EDGE), jnp.float32),
            jax.ShapeDtypeStruct((3, 16, 32, EDGE), jnp.bfloat16),
        ],
        scratch_shapes=[
            pltpu.VMEM((2, 1024, EDGE), jnp.float32),
            pltpu.VMEM((2, 128, EDGE), jnp.float32),
            pltpu.VMEM((3, 20, wide, EDGE), jnp.float32),
            pltpu.VMEM((3, 20, wide, EDGE), jnp.float32),
            pltpu.VMEM((3, 18, wide, EDGE), jnp.float32),
        ],
        compiler_params=pltpu.CompilerParams(vmem_limit_bytes=40 * 1024 * 1024),
    )(sums, low, high, right, fields)


def exchanged(block, axis, dim, width):
    count = lax.axis_size(axis)
    forward = [(i, i + 1) for i in range(count - 1)]
    backward = [(target, source) for source, target in forward]
    low = lax.ppermute(
        lax.slice_in_dim(block, block.shape[dim] - width, None, axis=dim), axis, forward
    )
    high = lax.ppermute(lax.slice_in_dim(block, 0, width, axis=dim), axis, backward)
    return low, high


def slot_ranks(destination, block_count):
    count = destination.shape[0]
    one_hot = (destination[:, None] == jnp.arange(block_count, dtype=jnp.int32)[None, :]).astype(
        jnp.bfloat16
    )
    positions = jnp.arange(count, dtype=jnp.int32)
    lower = (positions[:, None] > positions[None, :]).astype(jnp.bfloat16)
    before = jnp.dot(lower, one_hot, preferred_element_type=jnp.float32)
    return jnp.sum(before * one_hot.astype(jnp.float32), axis=1).astype(jnp.int32)


def arrival_places(destination, places, receiver, capacity):
    count = destination.shape[1]
    to_me = destination == receiver
    positions = jnp.arange(count, dtype=jnp.int32)
    upper = (positions[:, None] < positions[None, :]).astype(jnp.bfloat16)
    rank = jnp.dot(
        to_me.astype(jnp.bfloat16), upper, preferred_element_type=jnp.float32
    ).astype(jnp.int32)
    rank = jnp.where(to_me, rank, -1)
    matches = rank[:, None, :] == jnp.arange(capacity, dtype=jnp.int32)[None, :, None]
    return jnp.sum(jnp.where(matches, places[:, None, :], 0), axis=2).reshape(-1)


def shards(
    velocity,
    stretch,
    coupling,
    strengths,
    remesh,
    green_left,
    green_right,
    tile_owner,
    tile_place,
    row_dest,
    row_place,
):
    blocks = lax.axis_size("blk")
    spans = lax.axis_size("span")
    my_block = lax.axis_index("blk")
    my_span = lax.axis_index("span")
    tile_count = remesh.shape[0] // EDGE
    grid_count = velocity.shape[0] * velocity.shape[1] * velocity.shape[2]
    row_cap = 2 * grid_count // blocks

    pieces = tile_pieces(remesh, strengths, green_left)
    held = (
        velocity,
        stretch,
        coupling,
        tile_owner,
        tile_place,
        row_dest,
        row_place,
    )
    pieces, held = lax.optimization_barrier((pieces, held))
    velocity, stretch, coupling, tile_owner, tile_place, row_dest, row_place = held
    arrived = lax.all_to_all(pieces, "blk", split_axis=0, concat_axis=0, tiled=True)

    def mine(values, count):
        return lax.dynamic_index_in_dim(
            values.reshape(blocks, spans, count), my_span, 1, keepdims=False
        )

    owners = mine(tile_owner, tile_count).reshape(-1)
    places = mine(tile_place, tile_count).reshape(-1)
    position = owners * 12 + places
    entry = jnp.arange(16, dtype=jnp.int32)[None, :]
    block = jnp.arange(blocks, dtype=jnp.int32)[:, None]
    quarter = my_block // 16
    outer = jnp.where(
        quarter >= 2, (block - 1) * 12 + (entry - 12) * 4 + 3, (block + 1) * 12 + (entry - 12) * 4
    )
    outer_block = jnp.where(quarter >= 2, block - 1, block + 1)
    outer = jnp.where((outer_block >= 0) & (outer_block < blocks) & (entry < 15), outer, -1)
    wanted = jnp.where(entry < 12, block * 12 + entry, outer).reshape(-1)
    tile_picker = (wanted[:, None] == position[None, :]).astype(jnp.bfloat16)

    fields = jnp.concatenate([velocity, stretch, coupling[None]], axis=0)
    low, high = exchanged(fields, "blk", 1, REACH)
    fields = jnp.concatenate([low, fields, high], axis=1)
    low, high = exchanged(fields, "span", 2, REACH)
    blank = jnp.zeros(fields.shape[:2] + (SIDE - REACH, EDGE), fields.dtype)
    fields = jnp.concatenate([blank, low, fields, high, blank], axis=2)

    destinations = mine(row_dest, grid_count)
    row_places = mine(row_place, grid_count)
    dest_mine = lax.dynamic_index_in_dim(destinations, my_block, 0, keepdims=False)
    row_slot = dest_mine * row_cap + slot_ranks(dest_mine, blocks)
    row_spreader = (
        row_slot[None, :] == jnp.arange(blocks * row_cap, dtype=jnp.int32)[:, None]
    ).astype(jnp.bfloat16)
    row_where = arrival_places(destinations, row_places, my_block, row_cap)
    remesh_rows = gathered_rows(row_where, remesh)

    arrived, tile_picker, fields, row_spreader, remesh_rows = lax.optimization_barrier(
        (arrived, tile_picker, fields, row_spreader, remesh_rows)
    )
    sums = jnp.dot(
        tile_picker, arrived.reshape(-1, 2 * EDGE), preferred_element_type=jnp.float32
    ).astype(jnp.bfloat16)
    sums = lax.all_to_all(
        sums.reshape(blocks, 16, 2 * EDGE), "blk", split_axis=0, concat_axis=0, tiled=True
    )
    split = sums.reshape(4, 16, 16, 2 * EDGE)
    forward = [(i, i + 1) for i in range(spans - 1)]
    backward = [(i + 1, i) for i in range(spans - 1)]
    low = lax.ppermute(split[:, 14:16, :, EDGE:], "span", forward)
    high = lax.ppermute(split[:, 0:2, :, :EDGE], "span", backward)
    current, vorticity = grid_update(
        sums.reshape(-1, 2 * EDGE),
        low.reshape(-1, EDGE),
        high.reshape(-1, EDGE),
        green_right,
        fields,
    )
    outgoing = jnp.dot(
        row_spreader, vorticity.reshape(grid_count, EDGE), preferred_element_type=jnp.float32
    ).astype(jnp.bfloat16)
    incoming = lax.all_to_all(
        outgoing.reshape(blocks, row_cap, EDGE), "blk", split_axis=0, concat_axis=0, tiled=True
    )
    spread = lax.dot_general(
        remesh_rows,
        incoming.reshape(-1, EDGE),
        (((0,), (0,)), ((), ())),
        preferred_element_type=jnp.float32,
    )
    return current, (1.0 - blend) * strengths.astype(jnp.float32) + blend * spread


def solution(mesh):
    placed = (
        P(None, "blk", "span", None),
        P(None, "blk", "span", None),
        P("blk", "span", None),
        P(("blk", "span"), None),
        P(("blk", "span"), None),
        P(),
        P(),
        P(),
        P(),
        P(),
        P(),
    )
    return jax.shard_map(
        shards,
        mesh=mesh,
        in_specs=placed,
        out_specs=(P(None, "blk", "span", None), P(("blk", "span"), None)),
        check_vma=False,
    )
```

```python
import jax
import jax.numpy as jnp
from jax import lax
from jax.experimental import pallas as pl
from jax.experimental.pallas import tpu as pltpu
from jax.sharding import PartitionSpec as P

step_size = 0.05
viscosity = 0.4
blend = 0.5

EDGE = 128
REACH = 3
SIDE = 8
GROUP = 16


def pieces_kernel(remesh_ref, strengths_ref, left_ref, out_ref, scratch):
    vortex = jnp.dot(
        remesh_ref[...], strengths_ref[...], preferred_element_type=jnp.float32
    ).astype(jnp.bfloat16)
    left = left_ref[...]
    for pair in range(GROUP // 2):
        first = vortex[(2 * pair) * EDGE : (2 * pair + 1) * EDGE]
        second = vortex[(2 * pair + 1) * EDGE : (2 * pair + 2) * EDGE]
        both = jnp.dot(
            left, jnp.concatenate([first, second], axis=1), preferred_element_type=jnp.float32
        )
        for half in range(2):
            tile = 2 * pair + half
            for quarter in range(4):
                for side in range(2):
                    start = quarter * 32 + side * 16
                    scratch[
                        side, pl.ds(quarter * 16 * GROUP + tile, 16, stride=GROUP), :
                    ] = both[start : start + 16, half * EDGE : (half + 1) * EDGE]
    for side in range(2):
        out_ref[:, :, side * EDGE : (side + 1) * EDGE] = (
            scratch[side].astype(jnp.bfloat16).reshape(64, GROUP, EDGE)
        )


def tile_pieces(remesh, strengths, left):
    tiles = remesh.shape[0] // EDGE
    return pl.pallas_call(
        pieces_kernel,
        grid=(tiles // GROUP,),
        in_specs=[
            pl.BlockSpec((GROUP * EDGE, EDGE), lambda g: (g, 0)),
            pl.BlockSpec((EDGE, EDGE), lambda g: (0, 0)),
            pl.BlockSpec((EDGE, EDGE), lambda g: (0, 0)),
        ],
        out_specs=pl.BlockSpec((64, GROUP, 2 * EDGE), lambda g: (0, g, 0)),
        out_shape=jax.ShapeDtypeStruct((64, tiles, 2 * EDGE), jnp.bfloat16),
        scratch_shapes=[pltpu.VMEM((2, 64 * GROUP, EDGE), jnp.float32)],
        compiler_params=pltpu.CompilerParams(vmem_limit_bytes=60 * 1024 * 1024),
    )(remesh, strengths, left)


def gather_kernel(index_ref, remesh_ref, out_ref, wide, picked):
    wide[...] = remesh_ref[...].astype(jnp.float32)

    def some(step, carry):
        for k in range(16):
            slot = step * 16 + k
            picked[pl.ds(slot, 1), :] = wide[pl.ds(index_ref[slot], 1), :]
        return carry

    lax.fori_loop(0, out_ref.shape[0] // 16, some, 0)
    out_ref[...] = picked[...].astype(jnp.bfloat16)


def gathered_rows(index, remesh):
    slots = index.shape[0]
    return pl.pallas_call(
        gather_kernel,
        in_specs=[
            pl.BlockSpec(memory_space=pltpu.SMEM),
            pl.BlockSpec(memory_space=pltpu.VMEM),
        ],
        out_specs=pl.BlockSpec(memory_space=pltpu.VMEM),
        out_shape=jax.ShapeDtypeStruct((slots, EDGE), jnp.bfloat16),
        scratch_shapes=[
            pltpu.VMEM(remesh.shape, jnp.float32),
            pltpu.VMEM((slots, EDGE), jnp.float32),
        ],
        compiler_params=pltpu.CompilerParams(vmem_limit_bytes=40 * 1024 * 1024),
        cost_estimate=pl.CostEstimate(flops=0, bytes_accessed=16 * 1024 * 1024, transcendentals=0),
    )(index, remesh)


def sums_kernel(quarter_ref, position_ref, arrived_ref, out_ref, picker):
    quarter = quarter_ref[0]
    rows = picker.shape[0]
    row = lax.broadcasted_iota(jnp.int32, (rows, EDGE), 0)
    block = row // 16
    entry = row % 16
    late = quarter >= 2
    outer_block = jnp.where(late, block - 1, block + 1)
    outer = outer_block * 12 + (entry - 12) * 4 + jnp.where(late, 3, 0)
    usable = (outer_block >= 0) & (outer_block < 64) & (entry < 15)
    wanted = jnp.where(entry < 12, block * 12 + entry, jnp.where(usable, outer, -1))
    for chunk in range(picker.shape[1] // EDGE):
        lanes = slice(chunk * EDGE, (chunk + 1) * EDGE)
        picker[:, lanes] = (wanted == position_ref[:, lanes]).astype(jnp.bfloat16)
    out_ref[...] = jnp.dot(
        picker[...], arrived_ref[...], preferred_element_type=jnp.float32
    ).astype(jnp.bfloat16)


def tile_sums(quarter, position, arrived):
    tiles = arrived.shape[0]
    vmem = pl.BlockSpec(memory_space=pltpu.VMEM)
    return pl.pallas_call(
        sums_kernel,
        in_specs=[pl.BlockSpec(memory_space=pltpu.SMEM), vmem, vmem],
        out_specs=vmem,
        out_shape=jax.ShapeDtypeStruct((1024, 2 * EDGE), jnp.bfloat16),
        scratch_shapes=[pltpu.VMEM((1024, tiles), jnp.bfloat16)],
        compiler_params=pltpu.CompilerParams(vmem_limit_bytes=40 * 1024 * 1024),
    )(quarter, position, arrived)


def widen_kernel(velocity_ref, stretch_ref, coupling_ref, low_ref, high_ref, ext_ref, last_ref, first_ref):
    span = 32
    wide = span + 2 * SIDE
    source = [velocity_ref.at[c] for c in range(3)] + [stretch_ref.at[d] for d in range(3)]
    source.append(coupling_ref)
    for f in range(7):

        def one(layer, carry, f=f):
            ext_ref[f, layer, 0:SIDE, :] = jnp.zeros((SIDE, EDGE), jnp.float32)
            ext_ref[f, layer, SIDE + span : wide, :] = jnp.zeros((SIDE, EDGE), jnp.float32)
            ext_ref[f, layer, SIDE - REACH : SIDE, :] = low_ref[f, layer]
            ext_ref[f, layer, SIDE + span : SIDE + span + REACH, :] = high_ref[f, layer]
            ext_ref[f, layer, SIDE : SIDE + span, :] = source[f][layer]
            return carry

        lax.fori_loop(0, 16, one, 0)
    for f in range(7):
        depth = 3 if f < 3 else 2
        at = 3 * f if f < 3 else 9 + 2 * (f - 3)
        for k in range(depth):
            last_ref[at + k] = ext_ref[f, 16 - depth + k, 4 : wide - 4, :]
            first_ref[at + k] = ext_ref[f, k, 4 : wide - 4, :]


def widened(velocity, stretch, coupling, low, high):
    wide = 32 + 2 * SIDE
    vmem = pl.BlockSpec(memory_space=pltpu.VMEM)
    return pl.pallas_call(
        widen_kernel,
        in_specs=[vmem] * 5,
        out_specs=[vmem] * 3,
        out_shape=[
            jax.ShapeDtypeStruct((7, 16, wide, EDGE), jnp.float32),
            jax.ShapeDtypeStruct((17, wide - 8, EDGE), jnp.float32),
            jax.ShapeDtypeStruct((17, wide - 8, EDGE), jnp.float32),
        ],
        compiler_params=pltpu.CompilerParams(vmem_limit_bytes=32 * 1024 * 1024),
    )(velocity, stretch, coupling, low, high)


def moved(value, direction):
    wide = value.shape[0]
    if direction == 1:
        return pltpu.roll(value, wide - 1, 0), pltpu.roll(value, 1, 0)
    lanes = lax.broadcasted_iota(jnp.int32, value.shape, 1)
    ahead = jnp.where(lanes < EDGE - 1, pltpu.roll(value, EDGE - 1, 1), 0.0)
    behind = jnp.where(lanes > 0, pltpu.roll(value, 1, 1), 0.0)
    return ahead, behind


def unforced(source, at, stretch, rate):
    centre = [source[c, at] for c in range(3)]
    squares = [(step_size * viscosity) * s * s for s in stretch]
    carried = [(0.5 * step_size) * s * u for s, u in zip(stretch, centre)]
    results = []
    for c in range(3):
        value = centre[c]
        twice = 2.0 * value
        change = value - rate * value
        for d in range(3):
            if d == 0:
                ahead, behind = source[c, at + 1], source[c, at - 1]
            else:
                ahead, behind = moved(value, d)
            change = change + squares[d] * (ahead + behind - twice)
            change = change - carried[d] * (ahead - behind)
        results.append(change)
    return results


def prepare_kernel(ext_ref, low_ref, high_ref, base_ref, stretch_ref, rate_ref, wide_velocity):
    span = 32
    wide = span + 2 * SIDE
    blank = jnp.zeros((4, EDGE), jnp.float32)

    def padded(slab):
        return jnp.concatenate([blank, slab, blank], axis=0)

    for c in range(3):
        for k in range(3):
            wide_velocity[c, k] = padded(low_ref[3 * c + k])
            wide_velocity[c, 19 + k] = padded(high_ref[3 * c + k])
    for d in range(3):
        for k in range(2):
            stretch_ref[d, k] = padded(low_ref[9 + 2 * d + k])
            stretch_ref[d, 18 + k] = padded(high_ref[9 + 2 * d + k])
    for k in range(2):
        rate_ref[k] = padded(low_ref[15 + k])
        rate_ref[18 + k] = padded(high_ref[15 + k])

    def inner(layer, carry):
        for c in range(3):
            wide_velocity[c, layer + 3] = ext_ref[c, layer]
            stretch_ref[c, layer + 2] = ext_ref[3 + c, layer]
        rate_ref[layer + 2] = ext_ref[6, layer]
        return carry

    lax.fori_loop(0, 16, inner, 0)

    def step(layer, carry):
        results = unforced(
            wide_velocity, layer + 1, [stretch_ref[d, layer] for d in range(3)], rate_ref[layer]
        )
        for c in range(3):
            base_ref[c, layer] = results[c]
        return carry

    lax.fori_loop(0, 20, step, 0)


def prepared(ext, low, high):
    wide = 32 + 2 * SIDE
    vmem = pl.BlockSpec(memory_space=pltpu.VMEM)
    return pl.pallas_call(
        prepare_kernel,
        in_specs=[vmem] * 3,
        out_specs=[vmem] * 3,
        out_shape=[
            jax.ShapeDtypeStruct((3, 20, wide, EDGE), jnp.float32),
            jax.ShapeDtypeStruct((3, 20, wide, EDGE), jnp.float32),
            jax.ShapeDtypeStruct((20, wide, EDGE), jnp.float32),
        ],
        scratch_shapes=[pltpu.VMEM((3, 22, wide, EDGE), jnp.float32)],
        compiler_params=pltpu.CompilerParams(vmem_limit_bytes=32 * 1024 * 1024),
        cost_estimate=pl.CostEstimate(
            flops=30 * 1000 * 1000, bytes_accessed=8 * 1024 * 1024, transcendentals=0
        ),
    )(ext, low, high)


def grid_kernel(
    sums_ref,
    low_ref,
    high_ref,
    right_ref,
    base_ref,
    stretch_ref,
    rate_ref,
    next_ref,
    rows_ref,
    centre_sums,
    side_sums,
    target,
    first,
    second,
):
    right = right_ref[...]
    span = 32
    wide = span + 2 * SIDE
    for side in range(2):
        centre_sums[side] = jnp.dot(
            sums_ref[:, side * EDGE : (side + 1) * EDGE], right, preferred_element_type=jnp.float32
        )
    side_sums[0] = jnp.dot(low_ref[...], right, preferred_element_type=jnp.float32)
    side_sums[1] = jnp.dot(high_ref[...], right, preferred_element_type=jnp.float32)
    for component in range(3):
        for layer in range(20):
            chord = layer - 2
            quarter = chord % 4
            entry = component * 4 + chord // 4 if 0 <= chord < 16 else 12 + component
            for side in range(2):
                target[component, layer, SIDE + 16 * side : SIDE + 16 * side + 16, :] = centre_sums[
                    side, pl.ds(quarter * 256 + entry, 16, stride=16), :
                ]
            target[component, layer, SIDE - 2 : SIDE, :] = side_sums[
                0, pl.ds(quarter * 32 + entry, 2, stride=16), :
            ]
            target[component, layer, SIDE + span : SIDE + span + 2, :] = side_sums[
                1, pl.ds(quarter * 32 + entry, 2, stride=16), :
            ]

    def first_step(layer, carry):
        rate = rate_ref[layer]
        for c in range(3):
            first[c, layer] = base_ref[c, layer] + rate * target[c, layer]
        return carry

    lax.fori_loop(0, 20, first_step, 0)

    def second_step(layer, carry):
        rate = rate_ref[layer + 1]
        results = unforced(
            first, layer + 1, [stretch_ref[d, layer + 1] for d in range(3)], rate
        )
        for c in range(3):
            second[c, layer] = results[c] + rate * target[c, layer + 1]
        return carry

    lax.fori_loop(0, 18, second_step, 0)

    def curl(layer, carry):
        centre = [second[c, layer + 1] for c in range(3)]
        half = [0.5 * stretch_ref[d, layer + 2] for d in range(3)]

        def slope(d, c):
            if d == 0:
                return half[0] * (second[c, layer + 2] - second[c, layer])
            ahead, behind = moved(centre[c], d)
            return half[d] * (ahead - behind)

        parts = (
            slope(1, 2) - slope(2, 1),
            slope(2, 0) - slope(0, 2),
            slope(0, 1) - slope(1, 0),
        )
        for c in range(3):
            rows_ref[c, layer] = parts[c][SIDE : SIDE + span].astype(jnp.bfloat16)
            next_ref[c, layer] = centre[c][SIDE : SIDE + span]
        return carry

    lax.fori_loop(0, 16, curl, 0)


def grid_update(sums, low, high, right, base, stretch, rate):
    wide = 32 + 2 * SIDE
    vmem = pl.BlockSpec(memory_space=pltpu.VMEM)
    return pl.pallas_call(
        grid_kernel,
        in_specs=[vmem] * 7,
        out_specs=[vmem] * 2,
        out_shape=[
            jax.ShapeDtypeStruct((3, 16, 32, EDGE), jnp.float32),
            jax.ShapeDtypeStruct((3, 16, 32, EDGE), jnp.bfloat16),
        ],
        scratch_shapes=[
            pltpu.VMEM((2, 1024, EDGE), jnp.float32),
            pltpu.VMEM((2, 128, EDGE), jnp.float32),
            pltpu.VMEM((3, 20, wide, EDGE), jnp.float32),
            pltpu.VMEM((3, 20, wide, EDGE), jnp.float32),
            pltpu.VMEM((3, 18, wide, EDGE), jnp.float32),
        ],
        compiler_params=pltpu.CompilerParams(vmem_limit_bytes=32 * 1024 * 1024),
    )(sums, low, high, right, base, stretch, rate)


def chain(count):
    forward = [(i, i + 1) for i in range(count - 1)]
    return forward, [(target, source) for source, target in forward]


def slot_ranks(destination, block_count):
    count = destination.shape[0]
    one_hot = (destination[:, None] == jnp.arange(block_count, dtype=jnp.int32)[None, :]).astype(
        jnp.bfloat16
    )
    positions = jnp.arange(count, dtype=jnp.int32)
    lower = (positions[:, None] > positions[None, :]).astype(jnp.bfloat16)
    before = jnp.dot(lower, one_hot, preferred_element_type=jnp.float32)
    return jnp.sum(before * one_hot.astype(jnp.float32), axis=1).astype(jnp.int32)


def arrival_places(destination, places, receiver, capacity):
    count = destination.shape[1]
    to_me = destination == receiver
    positions = jnp.arange(count, dtype=jnp.int32)
    upper = (positions[:, None] < positions[None, :]).astype(jnp.bfloat16)
    rank = jnp.dot(
        to_me.astype(jnp.bfloat16), upper, preferred_element_type=jnp.float32
    ).astype(jnp.int32)
    rank = jnp.where(to_me, rank, -1)
    matches = rank[:, None, :] == jnp.arange(capacity, dtype=jnp.int32)[None, :, None]
    return jnp.sum(jnp.where(matches, places[:, None, :], 0), axis=2).reshape(-1)


def shards(
    velocity,
    stretch,
    coupling,
    strengths,
    remesh,
    green_left,
    green_right,
    tile_owner,
    tile_place,
    row_dest,
    row_place,
):
    blocks = lax.axis_size("blk")
    spans = lax.axis_size("span")
    my_block = lax.axis_index("blk")
    my_span = lax.axis_index("span")
    tile_count = remesh.shape[0] // EDGE
    grid_count = velocity.shape[0] * velocity.shape[1] * velocity.shape[2]
    row_cap = 2 * grid_count // blocks

    pieces = tile_pieces(remesh, strengths, green_left)
    held = (
        velocity,
        stretch,
        coupling,
        tile_owner,
        tile_place,
        row_dest,
        row_place,
    )
    pieces, held = lax.optimization_barrier((pieces, held))
    velocity, stretch, coupling, tile_owner, tile_place, row_dest, row_place = held
    arrived = lax.all_to_all(pieces, "blk", split_axis=0, concat_axis=0, tiled=True)

    def mine(values, count):
        rows = values.reshape(blocks, spans * count // EDGE, EDGE)
        if count >= EDGE:
            part = lax.dynamic_slice_in_dim(
                rows, my_span * (count // EDGE), count // EDGE, axis=1
            )
            return part.reshape(blocks, count)
        whole = rows.reshape(blocks, spans, count)
        return lax.dynamic_index_in_dim(whole, my_span, 1, keepdims=False)

    owners = mine(tile_owner.T, tile_count).reshape(1, -1)
    places = mine(tile_place, tile_count).reshape(1, -1)
    position = owners * 12 + places
    quarter = jnp.reshape(my_block // 16, (1,)).astype(jnp.int32)

    forward, backward = chain(spans)
    fields = (velocity, stretch, coupling[None])
    low = lax.ppermute(
        jnp.concatenate([f[:, :, -REACH:] for f in fields], axis=0), "span", forward
    )
    high = lax.ppermute(
        jnp.concatenate([f[:, :, :REACH] for f in fields], axis=0), "span", backward
    )
    extended, last, opening = widened(velocity, stretch, coupling, low, high)
    block_forward, block_backward = chain(blocks)
    low = lax.ppermute(last, "blk", block_forward)
    high = lax.ppermute(opening, "blk", block_backward)

    destinations = mine(row_dest.T, grid_count)
    row_places = mine(row_place, grid_count)
    dest_mine = lax.dynamic_index_in_dim(destinations, my_block, 0, keepdims=False)
    row_slot = dest_mine * row_cap + slot_ranks(dest_mine, blocks)
    row_spreader = (
        row_slot[None, :] == jnp.arange(blocks * row_cap, dtype=jnp.int32)[:, None]
    ).astype(jnp.bfloat16)
    row_where = arrival_places(destinations, row_places, my_block, row_cap)
    remesh_rows = gathered_rows(row_where, remesh)

    arrived, position, row_spreader, remesh_rows = lax.optimization_barrier(
        (arrived, position, row_spreader, remesh_rows)
    )
    sums = tile_sums(quarter, position, arrived.reshape(-1, 2 * EDGE))
    sums, extended, low, high = lax.optimization_barrier((sums, extended, low, high))
    base, wide_stretch, rate = prepared(extended, low, high)
    sums = lax.all_to_all(
        sums.reshape(blocks, 16, 2 * EDGE), "blk", split_axis=0, concat_axis=0, tiled=True
    )
    split = sums.reshape(4, 16, 16, 2 * EDGE)
    low = lax.ppermute(split[:, 14:16, :, EDGE:], "span", forward)
    high = lax.ppermute(split[:, 0:2, :, :EDGE], "span", backward)
    current, vorticity = grid_update(
        sums.reshape(-1, 2 * EDGE),
        low.reshape(-1, EDGE),
        high.reshape(-1, EDGE),
        green_right,
        base,
        wide_stretch,
        rate,
    )
    outgoing = jnp.dot(
        row_spreader, vorticity.reshape(grid_count, EDGE), preferred_element_type=jnp.float32
    ).astype(jnp.bfloat16)
    incoming = lax.all_to_all(
        outgoing.reshape(blocks, row_cap, EDGE), "blk", split_axis=0, concat_axis=0, tiled=True
    )
    spread = lax.dot_general(
        remesh_rows,
        incoming.reshape(-1, EDGE),
        (((0,), (0,)), ((), ())),
        preferred_element_type=jnp.float32,
    )
    return current, (1.0 - blend) * strengths.astype(jnp.float32) + blend * spread


def solution(mesh):
    placed = (
        P(None, "blk", "span", None),
        P(None, "blk", "span", None),
        P("blk", "span", None),
        P(("blk", "span"), None),
        P(("blk", "span"), None),
        P(),
        P(),
        P(),
        P(),
        P(),
        P(),
    )
    return jax.shard_map(
        shards,
        mesh=mesh,
        in_specs=placed,
        out_specs=(P(None, "blk", "span", None), P(("blk", "span"), None)),
        check_vma=False,
    )
```

```python
import jax
import jax.numpy as jnp
from jax import lax
from jax.experimental import pallas as pl
from jax.experimental.pallas import tpu as pltpu
from jax.sharding import PartitionSpec as P

step_size = 0.05
viscosity = 0.4
blend = 0.5

EDGE = 128
REACH = 3
FRONT = 9
WIDE = 48
SPAN = 32
GROUP = 32
PITCH = GROUP + 1
ROW_PITCH = 17


def twice_diagonal(block):
    blank = jnp.zeros_like(block)
    return jnp.concatenate(
        [jnp.concatenate([block, blank], axis=1), jnp.concatenate([blank, block], axis=1)], axis=0
    )


def pieces_kernel(remesh_ref, strengths_ref, left_ref, out_ref, scratch):
    left = left_ref[...]
    strengths = twice_diagonal(strengths_ref[...])
    for pair in range(GROUP // 2):
        first = remesh_ref[(2 * pair) * EDGE : (2 * pair + 1) * EDGE, :]
        second = remesh_ref[(2 * pair + 1) * EDGE : (2 * pair + 2) * EDGE, :]
        vortex = jnp.dot(
            jnp.concatenate([first, second], axis=1), strengths, preferred_element_type=jnp.float32
        ).astype(jnp.bfloat16)
        both = jnp.dot(left, vortex, preferred_element_type=jnp.float32)
        for half in range(2):
            tile = 2 * pair + half
            for quarter in range(4):
                for side in range(2):
                    start = quarter * 32 + side * 16
                    scratch[
                        side, pl.ds(quarter * 16 * PITCH + tile, 16, stride=PITCH), :
                    ] = both[start : start + 16, half * EDGE : (half + 1) * EDGE]
    for side in range(2):
        for piece in range(64):
            out_ref[piece, :, side * EDGE : (side + 1) * EDGE] = scratch[
                side, piece * PITCH : piece * PITCH + GROUP, :
            ].astype(jnp.bfloat16)


def tile_pieces(remesh, strengths, left):
    tiles = remesh.shape[0] // EDGE
    return pl.pallas_call(
        pieces_kernel,
        grid=(tiles // GROUP,),
        in_specs=[
            pl.BlockSpec((GROUP * EDGE, EDGE), lambda g: (g, 0)),
            pl.BlockSpec((EDGE, EDGE), lambda g: (0, 0)),
            pl.BlockSpec((EDGE, EDGE), lambda g: (0, 0)),
        ],
        out_specs=pl.BlockSpec((64, GROUP, 2 * EDGE), lambda g: (0, g, 0)),
        out_shape=jax.ShapeDtypeStruct((64, tiles, 2 * EDGE), jnp.bfloat16),
        scratch_shapes=[pltpu.VMEM((2, 64 * PITCH, EDGE), jnp.float32)],
        compiler_params=pltpu.CompilerParams(vmem_limit_bytes=60 * 1024 * 1024),
    )(remesh, strengths, left)


def gather_kernel(index_ref, remesh_ref, out_ref, wide, picked):
    wide[...] = remesh_ref[...].astype(jnp.float32)

    def some(step, carry):
        for k in range(16):
            slot = step * 16 + k
            picked[pl.ds(slot, 1), :] = wide[pl.ds(index_ref[slot], 1), :]
        return carry

    lax.fori_loop(0, out_ref.shape[0] // 16, some, 0)
    out_ref[...] = picked[...].astype(jnp.bfloat16)


def gathered_rows(index, remesh):
    slots = index.shape[0]
    return pl.pallas_call(
        gather_kernel,
        in_specs=[
            pl.BlockSpec(memory_space=pltpu.SMEM),
            pl.BlockSpec(memory_space=pltpu.VMEM),
        ],
        out_specs=pl.BlockSpec(memory_space=pltpu.VMEM),
        out_shape=jax.ShapeDtypeStruct((slots, EDGE), jnp.bfloat16),
        scratch_shapes=[
            pltpu.VMEM(remesh.shape, jnp.float32),
            pltpu.VMEM((slots, EDGE), jnp.float32),
        ],
        compiler_params=pltpu.CompilerParams(vmem_limit_bytes=16 * 1024 * 1024),
        cost_estimate=pl.CostEstimate(flops=0, bytes_accessed=16 * 1024 * 1024, transcendentals=0),
    )(index, remesh)


def sums_kernel(quarter_ref, position_ref, arrived_ref, out_ref):
    depth = 1024
    late = quarter_ref[0] >= 2
    row = lax.broadcasted_iota(jnp.int32, (out_ref.shape[0], EDGE), 0)
    block = row // 16
    entry = row % 16
    outer_block = jnp.where(late, block - 1, block + 1)
    outer = outer_block * 12 + (entry - 12) * 4 + jnp.where(late, 3, 0)
    usable = (outer_block >= 0) & (outer_block < 64) & (entry < 15)
    wanted = jnp.where(entry < 12, block * 12 + entry, jnp.where(usable, outer, -1))
    total = None
    for first in range(0, arrived_ref.shape[0], depth):
        picker = jnp.concatenate(
            [
                (wanted == position_ref[:, start : start + EDGE]).astype(jnp.bfloat16)
                for start in range(first, first + depth, EDGE)
            ],
            axis=1,
        )
        part = jnp.dot(
            picker, arrived_ref[first : first + depth, :], preferred_element_type=jnp.float32
        )
        total = part if total is None else total + part
    out_ref[...] = total.astype(jnp.bfloat16)


def tile_sums(quarter, position, arrived):
    vmem = pl.BlockSpec(memory_space=pltpu.VMEM)
    return pl.pallas_call(
        sums_kernel,
        in_specs=[pl.BlockSpec(memory_space=pltpu.SMEM), vmem, vmem],
        out_specs=vmem,
        out_shape=jax.ShapeDtypeStruct((1024, 2 * EDGE), jnp.bfloat16),
        compiler_params=pltpu.CompilerParams(vmem_limit_bytes=16 * 1024 * 1024),
    )(quarter, position, arrived)


def widen_kernel(velocity_ref, stretch_ref, coupling_ref, low_ref, high_ref, ext_ref, last_ref, first_ref):
    back = FRONT + SPAN
    source = [velocity_ref.at[c] for c in range(3)] + [stretch_ref.at[d] for d in range(3)]
    source.append(coupling_ref)
    for f in range(7):

        def one(layer, carry, f=f):
            ext_ref[f, layer, 0:8, :] = jnp.zeros((8, EDGE), jnp.float32)
            ext_ref[f, layer, WIDE - 8 : WIDE, :] = jnp.zeros((8, EDGE), jnp.float32)
            ext_ref[f, layer, FRONT - REACH : FRONT, :] = low_ref[f, layer]
            ext_ref[f, layer, back : back + REACH, :] = high_ref[f, layer]
            ext_ref[f, layer, FRONT:back, :] = source[f][layer]
            return carry

        lax.fori_loop(0, 16, one, 0)
    for f in range(7):
        depth = 3 if f < 3 else 2
        at = 3 * f if f < 3 else 9 + 2 * (f - 3)
        for k in range(depth):
            last_ref[at + k] = ext_ref[f, 16 - depth + k, 4 : WIDE - 4, :]
            first_ref[at + k] = ext_ref[f, k, 4 : WIDE - 4, :]


def widened(velocity, stretch, coupling, low, high):
    vmem = pl.BlockSpec(memory_space=pltpu.VMEM)
    return pl.pallas_call(
        widen_kernel,
        in_specs=[vmem] * 5,
        out_specs=[vmem] * 3,
        out_shape=[
            jax.ShapeDtypeStruct((7, 16, WIDE, EDGE), jnp.float32),
            jax.ShapeDtypeStruct((17, WIDE - 8, EDGE), jnp.float32),
            jax.ShapeDtypeStruct((17, WIDE - 8, EDGE), jnp.float32),
        ],
        compiler_params=pltpu.CompilerParams(vmem_limit_bytes=16 * 1024 * 1024),
    )(velocity, stretch, coupling, low, high)


def unforced(source, at, squares, halves, keep, lanes, low):
    whole = [source[c, at] for c in range(3)]
    centre = [value[low:] for value in whole]
    carried = [h * u for h, u in zip(halves, centre)]
    ahead_weight = [s - a for s, a in zip(squares, carried)]
    behind_weight = [s + a for s, a in zip(squares, carried)]
    ahead_weight[2] = jnp.where(lanes < EDGE - 1, ahead_weight[2], 0.0)
    behind_weight[2] = jnp.where(lanes > 0, behind_weight[2], 0.0)
    results = []
    for c in range(3):
        total = keep * centre[c]
        total = total + ahead_weight[0] * source[c, at + 1, low:, :]
        total = total + behind_weight[0] * source[c, at - 1, low:, :]
        total = total + ahead_weight[1] * pltpu.roll(whole[c], WIDE - 1, 0)[low:]
        total = total + behind_weight[1] * pltpu.roll(whole[c], 1, 0)[low:]
        total = total + ahead_weight[2] * pltpu.roll(centre[c], EDGE - 1, 1)
        total = total + behind_weight[2] * pltpu.roll(centre[c], 1, 1)
        results.append(total)
    return results


def entry_of(component, layer):
    chord = layer - 2
    entry = component * 4 + chord // 4 if 0 <= chord < 16 else 12 + component
    return chord % 4, entry


def front_kernel(
    sums_ref,
    right_ref,
    ext_ref,
    low_ref,
    high_ref,
    target_ref,
    base_ref,
    squares_ref,
    halves_ref,
    keep_ref,
    rate_ref,
    velocity,
    spread,
):
    blank = jnp.zeros((8, EDGE), jnp.float32)
    lanes = lax.broadcasted_iota(jnp.int32, (WIDE, EDGE), 1)
    product = jnp.dot(
        sums_ref[...], twice_diagonal(right_ref[...]), preferred_element_type=jnp.float32
    )
    for side in range(2):
        for piece in range(64):
            spread[side, piece * ROW_PITCH : piece * ROW_PITCH + 16, :] = product[
                piece * 16 : piece * 16 + 16, side * EDGE : (side + 1) * EDGE
            ]

    def padded(slab):
        return jnp.concatenate([blank[:4], slab, blank[:4]], axis=0)

    for c in range(3):
        for k in range(3):
            velocity[c, k] = padded(low_ref[3 * c + k])
            velocity[c, 19 + k] = padded(high_ref[3 * c + k])
        for layer in range(16):
            velocity[c, layer + 3] = ext_ref[c, layer]

    for layer in range(20):
        inner = layer - 2
        if 0 <= inner < 16:
            stretch = [ext_ref[3 + d, inner] for d in range(3)]
            rate = ext_ref[6, inner]
        else:
            slab, k = (low_ref, layer) if inner < 0 else (high_ref, inner - 16)
            stretch = [padded(slab[9 + 2 * d + k]) for d in range(3)]
            rate = padded(slab[15 + k])
        squares = [(step_size * viscosity) * s * s for s in stretch]
        halves = [(0.5 * step_size) * s for s in stretch]
        keep = 1.0 - rate - 2.0 * (squares[0] + squares[1] + squares[2])
        results = unforced(velocity, layer + 1, squares, halves, keep, lanes, 0)
        for d in range(3):
            squares_ref[d, layer] = squares[d]
            halves_ref[d, layer] = halves[d]
            base_ref[d, layer] = results[d]
        keep_ref[layer] = keep
        rate_ref[layer] = rate
        for component in range(3):
            quarter, entry = entry_of(component, layer)
            target_ref[component, layer, 0:8, :] = blank
            target_ref[component, layer, WIDE - 8 : WIDE, :] = blank
            for side in range(2):
                start = FRONT + 16 * side
                target_ref[component, layer, start : start + 16, :] = spread[
                    side, pl.ds(quarter * 16 * ROW_PITCH + entry, 16, stride=ROW_PITCH), :
                ]
            target_ref[component, layer, 8:FRONT, :] = blank[: FRONT - 8]


def fronted(sums, right, ext, low, high):
    vmem = pl.BlockSpec(memory_space=pltpu.VMEM)
    return pl.pallas_call(
        front_kernel,
        in_specs=[vmem] * 5,
        out_specs=[vmem] * 6,
        out_shape=[jax.ShapeDtypeStruct((3, 20, WIDE, EDGE), jnp.float32)] * 4
        + [jax.ShapeDtypeStruct((20, WIDE, EDGE), jnp.float32)] * 2,
        scratch_shapes=[
            pltpu.VMEM((3, 22, WIDE, EDGE), jnp.float32),
            pltpu.VMEM((2, 64 * ROW_PITCH, EDGE), jnp.float32),
        ],
        compiler_params=pltpu.CompilerParams(vmem_limit_bytes=16 * 1024 * 1024),
        cost_estimate=pl.CostEstimate(
            flops=164 * 1000 * 1000, bytes_accessed=8 * 1024 * 1024, transcendentals=0
        ),
    )(sums, right, ext, low, high)


def grid_kernel(
    target_ref,
    low_ref,
    high_ref,
    right_ref,
    base_ref,
    squares_ref,
    halves_ref,
    keep_ref,
    rate_ref,
    slot_ref,
    next_ref,
    out_ref,
    side_sums,
    forced,
    first,
    second,
    rows,
    slots,
    done,
    sems,
):
    right = right_ref[...]
    back = FRONT + SPAN
    lanes = lax.broadcasted_iota(jnp.int32, (WIDE - 8, EDGE), 1)
    side_sums[0] = jnp.dot(low_ref[...], right, preferred_element_type=jnp.float32)
    side_sums[1] = jnp.dot(high_ref[...], right, preferred_element_type=jnp.float32)
    slots[...] = jnp.zeros_like(slots)
    for c in range(3):
        for layer in range(20):
            quarter, entry = entry_of(c, layer)
            forced[c, layer] = target_ref[c, layer]
            forced[c, layer, FRONT - 2 : FRONT, :] = side_sums[
                0, pl.ds(quarter * 32 + entry, 2, stride=16), :
            ]
            forced[c, layer, back : back + 2, :] = side_sums[
                1, pl.ds(quarter * 32 + entry, 2, stride=16), :
            ]
    for layer in range(20):
        rate = rate_ref[layer]
        for c in range(3):
            pull = rate * forced[c, layer]
            forced[c, layer] = pull
            first[c, layer] = base_ref[c, layer] + pull

    def second_step(layer):
        results = unforced(
            first,
            layer + 1,
            [squares_ref[d, layer + 1, 8:, :] for d in range(3)],
            [halves_ref[d, layer + 1, 8:, :] for d in range(3)],
            keep_ref[layer + 1, 8:, :],
            lanes,
            8,
        )
        for c in range(3):
            second[c, layer] = results[c] + forced[c, layer + 1, 8:, :]

    def curl(layer):
        whole = [second[c, layer + 1] for c in range(3)]
        half = [halves_ref[d, layer + 2, 8:, :] for d in range(3)]

        def slope(d, c):
            if d == 0:
                return half[0] * (second[c, layer + 2] - second[c, layer])
            if d == 1:
                ahead = pltpu.roll(whole[c], WIDE - 9, 0)
                behind = pltpu.roll(whole[c], 1, 0)
            else:
                ahead = jnp.where(lanes < EDGE - 1, pltpu.roll(whole[c], EDGE - 1, 1), 0.0)
                behind = jnp.where(lanes > 0, pltpu.roll(whole[c], 1, 1), 0.0)
            return half[d] * (ahead - behind)

        parts = (
            slope(1, 2) - slope(2, 1),
            slope(2, 0) - slope(0, 2),
            slope(0, 1) - slope(1, 0),
        )
        for c in range(3):
            start = (c * 16 + layer) * SPAN
            rows[start : start + SPAN, :] = (1.0 / step_size) * parts[c][1 : 1 + SPAN]
            done[c, layer] = whole[c][1 : 1 + SPAN]

    def scatter(layer):
        for c in range(3):
            start = (c * 16 + layer) * SPAN
            for row in range(start, start + SPAN):
                slots[pl.ds(slot_ref[row], 1), :] = rows[row : row + 1, :]

    copies = []
    for layer in range(18):
        second_step(layer)
        if layer >= 2:
            curl(layer - 2)
            scatter(layer - 2)
        if layer in (9, 17):
            part = len(copies)
            copies.append(
                pltpu.make_async_copy(
                    done.at[:, pl.ds(8 * part, 8)], next_ref.at[:, pl.ds(8 * part, 8)], sems.at[part]
                )
            )
            copies[part].start()
    out_ref[...] = slots[...].astype(jnp.bfloat16)
    for copy in copies:
        copy.wait()


def grid_update(target, low, high, right, base, squares, halves, keep, rate, slot):
    vmem = pl.BlockSpec(memory_space=pltpu.VMEM)
    return pl.pallas_call(
        grid_kernel,
        in_specs=[vmem] * 9 + [pl.BlockSpec(memory_space=pltpu.SMEM)],
        out_specs=[pl.BlockSpec(memory_space=pl.ANY), vmem],
        out_shape=[
            jax.ShapeDtypeStruct((3, 16, SPAN, EDGE), jnp.float32),
            jax.ShapeDtypeStruct((2 * slot.shape[0], EDGE), jnp.bfloat16),
        ],
        scratch_shapes=[
            pltpu.VMEM((2, 128, EDGE), jnp.float32),
            pltpu.VMEM((3, 20, WIDE, EDGE), jnp.float32),
            pltpu.VMEM((3, 20, WIDE, EDGE), jnp.float32),
            pltpu.VMEM((3, 18, WIDE - 8, EDGE), jnp.float32),
            pltpu.VMEM((slot.shape[0], EDGE), jnp.float32),
            pltpu.VMEM((2 * slot.shape[0], EDGE), jnp.float32),
            pltpu.VMEM((3, 16, SPAN, EDGE), jnp.float32),
            pltpu.SemaphoreType.DMA((2,)),
        ],
        compiler_params=pltpu.CompilerParams(vmem_limit_bytes=24 * 1024 * 1024),
    )(target, low, high, right, base, squares, halves, keep, rate, slot)


def chain(count):
    forward = [(i, i + 1) for i in range(count - 1)]
    return forward, [(target, source) for source, target in forward]


def slot_ranks(destination, block_count):
    count = destination.shape[0]
    one_hot = (destination[:, None] == jnp.arange(block_count, dtype=jnp.int32)[None, :]).astype(
        jnp.bfloat16
    )
    positions = jnp.arange(count, dtype=jnp.int32)
    lower = (positions[:, None] > positions[None, :]).astype(jnp.bfloat16)
    before = jnp.dot(lower, one_hot, preferred_element_type=jnp.float32)
    return jnp.sum(before * one_hot.astype(jnp.float32), axis=1).astype(jnp.int32)


def arrival_places(destination, places, receiver, capacity):
    count = destination.shape[1]
    to_me = destination == receiver
    positions = jnp.arange(count, dtype=jnp.int32)
    upper = (positions[:, None] < positions[None, :]).astype(jnp.bfloat16)
    rank = jnp.dot(
        to_me.astype(jnp.bfloat16), upper, preferred_element_type=jnp.float32
    ).astype(jnp.int32)
    rank = jnp.where(to_me, rank, -1)
    matches = rank[:, None, :] == jnp.arange(capacity, dtype=jnp.int32)[None, :, None]
    return jnp.sum(jnp.where(matches, places[:, None, :], 0), axis=2).reshape(-1)


def shards(
    velocity,
    stretch,
    coupling,
    strengths,
    remesh,
    green_left,
    green_right,
    tile_owner,
    tile_place,
    row_dest,
    row_place,
):
    blocks = lax.axis_size("blk")
    spans = lax.axis_size("span")
    my_block = lax.axis_index("blk")
    my_span = lax.axis_index("span")
    tile_count = remesh.shape[0] // EDGE
    grid_count = velocity.shape[0] * velocity.shape[1] * velocity.shape[2]
    row_cap = 2 * grid_count // blocks

    pieces = tile_pieces(remesh, strengths, green_left)
    held = (
        velocity,
        stretch,
        coupling,
        tile_owner,
        tile_place,
        row_dest,
        row_place,
    )
    pieces, held = lax.optimization_barrier((pieces, held))
    velocity, stretch, coupling, tile_owner, tile_place, row_dest, row_place = held
    arrived = lax.all_to_all(pieces, "blk", split_axis=0, concat_axis=0, tiled=True)

    def mine(values, count):
        rows = values.reshape(blocks, spans * count // EDGE, EDGE)
        if count >= EDGE:
            part = lax.dynamic_slice_in_dim(
                rows, my_span * (count // EDGE), count // EDGE, axis=1
            )
            return part.reshape(blocks, count)
        whole = rows.reshape(blocks, spans, count)
        return lax.dynamic_index_in_dim(whole, my_span, 1, keepdims=False)

    owners = mine(tile_owner.T, tile_count).reshape(1, -1)
    places = mine(tile_place, tile_count).reshape(1, -1)
    position = owners * 12 + places
    quarter = jnp.reshape(my_block // 16, (1,)).astype(jnp.int32)

    forward, backward = chain(spans)
    fields = (velocity, stretch, coupling[None])
    low = lax.ppermute(
        jnp.concatenate([f[:, :, -REACH:] for f in fields], axis=0), "span", forward
    )
    high = lax.ppermute(
        jnp.concatenate([f[:, :, :REACH] for f in fields], axis=0), "span", backward
    )
    extended, last, opening = widened(velocity, stretch, coupling, low, high)
    block_forward, block_backward = chain(blocks)
    low = lax.ppermute(last, "blk", block_forward)
    high = lax.ppermute(opening, "blk", block_backward)

    destinations = mine(row_dest.T, grid_count)
    row_places = mine(row_place, grid_count)
    dest_mine = lax.dynamic_index_in_dim(destinations, my_block, 0, keepdims=False)
    row_slot = dest_mine * row_cap + slot_ranks(dest_mine, blocks)
    row_where = arrival_places(destinations, row_places, my_block, row_cap)
    remesh_rows = gathered_rows(row_where, remesh)

    arrived, position, row_slot, remesh_rows = lax.optimization_barrier(
        (arrived, position, row_slot, remesh_rows)
    )
    sums = tile_sums(quarter, position, arrived.reshape(-1, 2 * EDGE))
    sums, extended, low, high = lax.optimization_barrier((sums, extended, low, high))
    sums = lax.all_to_all(
        sums.reshape(blocks, 16, 2 * EDGE), "blk", split_axis=0, concat_axis=0, tiled=True
    )
    split = sums.reshape(4, 16, 16, 2 * EDGE)
    target, base, squares, halves, keep, rate = fronted(
        sums.reshape(-1, 2 * EDGE), green_right, extended, low, high
    )
    low = lax.ppermute(split[:, 14:16, :, EDGE:], "span", forward)
    high = lax.ppermute(split[:, 0:2, :, :EDGE], "span", backward)
    current, outgoing = grid_update(
        target,
        low.reshape(-1, EDGE),
        high.reshape(-1, EDGE),
        green_right,
        base,
        squares,
        halves,
        keep,
        rate,
        row_slot,
    )
    incoming = lax.all_to_all(
        outgoing.reshape(blocks, row_cap, EDGE), "blk", split_axis=0, concat_axis=0, tiled=True
    )
    spread = lax.dot_general(
        remesh_rows,
        incoming.reshape(-1, EDGE),
        (((0,), (0,)), ((), ())),
        preferred_element_type=jnp.float32,
    )
    return current, (1.0 - blend) * strengths.astype(jnp.float32) + blend * spread


def solution(mesh):
    placed = (
        P(None, "blk", "span", None),
        P(None, "blk", "span", None),
        P("blk", "span", None),
        P(("blk", "span"), None),
        P(("blk", "span"), None),
        P(),
        P(),
        P(),
        P(),
        P(),
        P(),
    )
    return jax.shard_map(
        shards,
        mesh=mesh,
        in_specs=placed,
        out_specs=(P(None, "blk", "span", None), P(("blk", "span"), None)),
        check_vma=False,
    )
```

```python
import jax
import jax.numpy as jnp
from jax import lax
from jax.experimental import pallas as pl
from jax.experimental.pallas import tpu as pltpu
from jax.sharding import PartitionSpec as P

step_size = 0.05
viscosity = 0.4
blend = 0.5

EDGE = 128
REACH = 3
FRONT = 4
WIDE = 40
SPAN = 32
GROUP = 32
PITCH = GROUP + 1
ROW_PITCH = 17


def twice_diagonal(block):
    blank = jnp.zeros_like(block)
    return jnp.concatenate(
        [jnp.concatenate([block, blank], axis=1), jnp.concatenate([blank, block], axis=1)], axis=0
    )


def pieces_kernel(remesh_ref, strengths_ref, left_ref, out_ref, scratch):
    left = left_ref[...]
    strengths = twice_diagonal(strengths_ref[...])
    paired = jnp.concatenate(
        [
            jnp.concatenate(
                [remesh_ref[at : at + EDGE, :], remesh_ref[at + EDGE : at + 2 * EDGE, :]], axis=1
            )
            for at in range(0, GROUP * EDGE, 2 * EDGE)
        ],
        axis=0,
    )
    vortex = jnp.dot(paired, strengths, preferred_element_type=jnp.float32).astype(jnp.bfloat16)
    for pair in range(GROUP // 2):
        both = jnp.dot(
            left, vortex[pair * EDGE : (pair + 1) * EDGE], preferred_element_type=jnp.float32
        )
        for half in range(2):
            tile = 2 * pair + half
            for quarter in range(4):
                for side in range(2):
                    start = quarter * 32 + side * 16
                    scratch[
                        side, pl.ds(quarter * 16 * PITCH + tile, 16, stride=PITCH), :
                    ] = both[start : start + 16, half * EDGE : (half + 1) * EDGE]
    for side in range(2):
        for piece in range(64):
            out_ref[piece, :, side * EDGE : (side + 1) * EDGE] = scratch[
                side, piece * PITCH : piece * PITCH + GROUP, :
            ].astype(jnp.bfloat16)


def tile_pieces(remesh, strengths, left):
    tiles = remesh.shape[0] // EDGE
    return pl.pallas_call(
        pieces_kernel,
        grid=(tiles // GROUP,),
        in_specs=[
            pl.BlockSpec((GROUP * EDGE, EDGE), lambda g: (g, 0)),
            pl.BlockSpec((EDGE, EDGE), lambda g: (0, 0)),
            pl.BlockSpec((EDGE, EDGE), lambda g: (0, 0)),
        ],
        out_specs=pl.BlockSpec((64, GROUP, 2 * EDGE), lambda g: (0, g, 0)),
        out_shape=jax.ShapeDtypeStruct((64, tiles, 2 * EDGE), jnp.bfloat16),
        scratch_shapes=[pltpu.VMEM((2, 64 * PITCH, EDGE), jnp.float32)],
        compiler_params=pltpu.CompilerParams(vmem_limit_bytes=60 * 1024 * 1024),
    )(remesh, strengths, left)


def gather_kernel(index_ref, remesh_ref, out_ref, wide, picked):
    wide[...] = remesh_ref[...].astype(jnp.float32)

    def some(step, carry):
        for k in range(16):
            slot = step * 16 + k
            picked[pl.ds(slot, 1), :] = wide[pl.ds(index_ref[slot], 1), :]
        return carry

    lax.fori_loop(0, out_ref.shape[0] // 16, some, 0)
    out_ref[...] = picked[...].astype(jnp.bfloat16)


def gathered_rows(index, remesh):
    slots = index.shape[0]
    return pl.pallas_call(
        gather_kernel,
        in_specs=[
            pl.BlockSpec(memory_space=pltpu.SMEM),
            pl.BlockSpec(memory_space=pltpu.VMEM),
        ],
        out_specs=pl.BlockSpec(memory_space=pltpu.VMEM),
        out_shape=jax.ShapeDtypeStruct((slots, EDGE), jnp.bfloat16),
        scratch_shapes=[
            pltpu.VMEM(remesh.shape, jnp.float32),
            pltpu.VMEM((slots, EDGE), jnp.float32),
        ],
        compiler_params=pltpu.CompilerParams(vmem_limit_bytes=16 * 1024 * 1024),
        cost_estimate=pl.CostEstimate(flops=0, bytes_accessed=16 * 1024 * 1024, transcendentals=0),
    )(index, remesh)


def sums_kernel(quarter_ref, position_ref, arrived_ref, out_ref, spread):
    depth = 1024
    blocks = 64
    row = lax.broadcasted_iota(jnp.int32, (12 * blocks, EDGE), 0)
    wanted = (row % blocks) * 12 + row // blocks
    total = None
    for first in range(0, arrived_ref.shape[0], depth):
        picker = jnp.concatenate(
            [
                (wanted == position_ref[:, start : start + EDGE]).astype(jnp.bfloat16)
                for start in range(first, first + depth, EDGE)
            ],
            axis=1,
        )
        part = jnp.dot(
            picker, arrived_ref[first : first + depth, :], preferred_element_type=jnp.float32
        )
        total = part if total is None else total + part
    late = quarter_ref[0] >= 2
    block = lax.broadcasted_iota(jnp.int32, (blocks, EDGE), 0)
    for side in range(2):
        lanes = slice(side * EDGE, (side + 1) * EDGE)
        places = [total[p * blocks : (p + 1) * blocks, lanes] for p in range(12)]
        for component in range(3):
            before = pltpu.roll(places[component * 4 + 3], 1, 0)
            after = pltpu.roll(places[component * 4], blocks - 1, 0)
            places.append(
                jnp.where(
                    late,
                    jnp.where(block > 0, before, 0.0),
                    jnp.where(block < blocks - 1, after, 0.0),
                )
            )
        places.append(jnp.zeros((blocks, EDGE), jnp.float32))
        for entry, value in enumerate(places):
            spread[side, pl.ds(entry, blocks, stride=ROW_PITCH), :] = value
        for k in range(blocks):
            out_ref[16 * k : 16 * k + 16, lanes] = spread[
                side, ROW_PITCH * k : ROW_PITCH * k + 16, :
            ].astype(jnp.bfloat16)


def tile_sums(quarter, position, arrived):
    vmem = pl.BlockSpec(memory_space=pltpu.VMEM)
    return pl.pallas_call(
        sums_kernel,
        in_specs=[pl.BlockSpec(memory_space=pltpu.SMEM), vmem, vmem],
        out_specs=vmem,
        out_shape=jax.ShapeDtypeStruct((1024, 2 * EDGE), jnp.bfloat16),
        scratch_shapes=[pltpu.VMEM((2, 64 * ROW_PITCH, EDGE), jnp.float32)],
        compiler_params=pltpu.CompilerParams(vmem_limit_bytes=16 * 1024 * 1024),
    )(quarter, position, arrived)


def widen_kernel(velocity_ref, stretch_ref, coupling_ref, low_ref, high_ref, wide_u, wide_s, wide_r, last_ref, first_ref):
    back = FRONT + SPAN
    source = [velocity_ref.at[c] for c in range(3)] + [stretch_ref.at[d] for d in range(3)]
    source.append(coupling_ref)
    wide = [wide_u.at[c] for c in range(3)] + [wide_s.at[d] for d in range(3)] + [wide_r]
    for f in range(7):

        def one(layer, carry, f=f):
            wide[f][layer, 0:8, :] = jnp.zeros((8, EDGE), jnp.float32)
            wide[f][layer, WIDE - 8 : WIDE, :] = jnp.zeros((8, EDGE), jnp.float32)
            wide[f][layer, FRONT - REACH : FRONT, :] = low_ref[f, layer]
            wide[f][layer, back : back + REACH, :] = high_ref[f, layer]
            wide[f][layer, FRONT:back, :] = source[f][layer]
            return carry

        lax.fori_loop(0, 16, one, 0)
    for f in range(7):
        depth = 3 if f < 3 else 2
        at = 3 * f if f < 3 else 9 + 2 * (f - 3)
        for k in range(depth):
            last_ref[at + k] = wide[f][16 - depth + k]
            first_ref[at + k] = wide[f][k]


def widened(velocity, stretch, coupling, low, high):
    vmem = pl.BlockSpec(memory_space=pltpu.VMEM)
    return pl.pallas_call(
        widen_kernel,
        in_specs=[vmem] * 5,
        out_specs=[vmem] * 5,
        out_shape=[
            jax.ShapeDtypeStruct((3, 16, WIDE, EDGE), jnp.float32),
            jax.ShapeDtypeStruct((3, 16, WIDE, EDGE), jnp.float32),
            jax.ShapeDtypeStruct((16, WIDE, EDGE), jnp.float32),
            jax.ShapeDtypeStruct((17, WIDE, EDGE), jnp.float32),
            jax.ShapeDtypeStruct((17, WIDE, EDGE), jnp.float32),
        ],
        compiler_params=pltpu.CompilerParams(vmem_limit_bytes=16 * 1024 * 1024),
    )(velocity, stretch, coupling, low, high)


def unforced(source, at, squares, halves, keep, lanes):
    centre = [source[c, at] for c in range(3)]
    carried = [h * u for h, u in zip(halves, centre)]
    ahead_weight = [s - a for s, a in zip(squares, carried)]
    behind_weight = [s + a for s, a in zip(squares, carried)]
    ahead_weight[2] = jnp.where(lanes < EDGE - 1, ahead_weight[2], 0.0)
    behind_weight[2] = jnp.where(lanes > 0, behind_weight[2], 0.0)
    results = []
    for c in range(3):
        total = keep * centre[c]
        total = total + ahead_weight[0] * source[c, at + 1]
        total = total + behind_weight[0] * source[c, at - 1]
        total = total + ahead_weight[1] * pltpu.roll(centre[c], WIDE - 1, 0)
        total = total + behind_weight[1] * pltpu.roll(centre[c], 1, 0)
        total = total + ahead_weight[2] * pltpu.roll(centre[c], EDGE - 1, 1)
        total = total + behind_weight[2] * pltpu.roll(centre[c], 1, 1)
        results.append(total)
    return results


def entry_of(component, layer):
    chord = layer - 2
    entry = component * 4 + chord // 4 if 0 <= chord < 16 else 12 + component
    return chord % 4, entry


def front_kernel(
    sums_ref,
    right_ref,
    wide_u,
    wide_s,
    wide_r,
    low_ref,
    high_ref,
    target_ref,
    base_ref,
    squares_ref,
    halves_ref,
    keep_ref,
    rate_ref,
    velocity,
    spread,
):
    blank = jnp.zeros((8, EDGE), jnp.float32)
    lanes = lax.broadcasted_iota(jnp.int32, (WIDE, EDGE), 1)
    product = jnp.dot(
        sums_ref[...], twice_diagonal(right_ref[...]), preferred_element_type=jnp.float32
    )
    for side in range(2):
        for piece in range(64):
            spread[side, piece * ROW_PITCH : piece * ROW_PITCH + 16, :] = product[
                piece * 16 : piece * 16 + 16, side * EDGE : (side + 1) * EDGE
            ]

    for c in range(3):
        for k in range(3):
            velocity[c, k] = low_ref[3 * c + k]
            velocity[c, 19 + k] = high_ref[3 * c + k]
        for layer in range(16):
            velocity[c, layer + 3] = wide_u[c, layer]

    for layer in range(20):
        inner = layer - 2
        if 0 <= inner < 16:
            stretch = [wide_s[d, inner] for d in range(3)]
            rate = wide_r[inner]
        else:
            slab, k = (low_ref, layer) if inner < 0 else (high_ref, inner - 16)
            stretch = [slab[9 + 2 * d + k] for d in range(3)]
            rate = slab[15 + k]
        squares = [(step_size * viscosity) * s * s for s in stretch]
        halves = [(0.5 * step_size) * s for s in stretch]
        keep = 1.0 - rate - 2.0 * (squares[0] + squares[1] + squares[2])
        results = unforced(velocity, layer + 1, squares, halves, keep, lanes)
        for d in range(3):
            squares_ref[d, layer] = squares[d]
            halves_ref[d, layer] = halves[d]
            base_ref[d, layer] = results[d]
        keep_ref[layer] = keep
        rate_ref[layer] = rate
        for component in range(3):
            quarter, entry = entry_of(component, layer)
            target_ref[component, layer, 0:8, :] = blank
            target_ref[component, layer, WIDE - 8 : WIDE, :] = blank
            for side in range(2):
                start = FRONT + 16 * side
                target_ref[component, layer, start : start + 16, :] = spread[
                    side, pl.ds(quarter * 16 * ROW_PITCH + entry, 16, stride=ROW_PITCH), :
                ]


def fronted(sums, right, fields, low, high):
    vmem = pl.BlockSpec(memory_space=pltpu.VMEM)
    return pl.pallas_call(
        front_kernel,
        in_specs=[vmem] * 7,
        out_specs=[vmem] * 6,
        out_shape=[jax.ShapeDtypeStruct((3, 20, WIDE, EDGE), jnp.float32)] * 4
        + [jax.ShapeDtypeStruct((20, WIDE, EDGE), jnp.float32)] * 2,
        scratch_shapes=[
            pltpu.VMEM((3, 22, WIDE, EDGE), jnp.float32),
            pltpu.VMEM((2, 64 * ROW_PITCH, EDGE), jnp.float32),
        ],
        compiler_params=pltpu.CompilerParams(vmem_limit_bytes=16 * 1024 * 1024),
        cost_estimate=pl.CostEstimate(
            flops=164 * 1000 * 1000, bytes_accessed=8 * 1024 * 1024, transcendentals=0
        ),
    )(sums, right, *fields, low, high)


def grid_kernel(
    target_ref,
    low_ref,
    high_ref,
    right_ref,
    base_ref,
    squares_ref,
    halves_ref,
    keep_ref,
    rate_ref,
    slot_ref,
    next_ref,
    out_ref,
    side_sums,
    forced,
    first,
    second,
    rows,
    slots,
    done,
    sems,
):
    right = right_ref[...]
    back = FRONT + SPAN
    lanes = lax.broadcasted_iota(jnp.int32, (WIDE, EDGE), 1)
    side_sums[0] = jnp.dot(low_ref[...], right, preferred_element_type=jnp.float32)
    side_sums[1] = jnp.dot(high_ref[...], right, preferred_element_type=jnp.float32)
    slots[...] = jnp.zeros_like(slots)
    for c in range(3):
        for layer in range(20):
            quarter, entry = entry_of(c, layer)
            forced[c, layer] = target_ref[c, layer]
            forced[c, layer, FRONT - 2 : FRONT, :] = side_sums[
                0, pl.ds(quarter * 32 + entry, 2, stride=16), :
            ]
            forced[c, layer, back : back + 2, :] = side_sums[
                1, pl.ds(quarter * 32 + entry, 2, stride=16), :
            ]
    for layer in range(20):
        rate = rate_ref[layer]
        for c in range(3):
            pull = rate * forced[c, layer]
            forced[c, layer] = pull
            first[c, layer] = base_ref[c, layer] + pull

    def second_step(layer):
        results = unforced(
            first,
            layer + 1,
            [squares_ref[d, layer + 1] for d in range(3)],
            [halves_ref[d, layer + 1] for d in range(3)],
            keep_ref[layer + 1],
            lanes,
        )
        for c in range(3):
            second[c, layer] = results[c] + forced[c, layer + 1]

    def curl(layer):
        whole = [second[c, layer + 1] for c in range(3)]
        half = [halves_ref[d, layer + 2] for d in range(3)]

        def slope(d, c):
            if d == 0:
                return half[0] * (second[c, layer + 2] - second[c, layer])
            if d == 1:
                ahead = pltpu.roll(whole[c], WIDE - 1, 0)
                behind = pltpu.roll(whole[c], 1, 0)
            else:
                ahead = jnp.where(lanes < EDGE - 1, pltpu.roll(whole[c], EDGE - 1, 1), 0.0)
                behind = jnp.where(lanes > 0, pltpu.roll(whole[c], 1, 1), 0.0)
            return half[d] * (ahead - behind)

        parts = (
            slope(1, 2) - slope(2, 1),
            slope(2, 0) - slope(0, 2),
            slope(0, 1) - slope(1, 0),
        )
        for c in range(3):
            start = (c * 16 + layer) * SPAN
            rows[start : start + SPAN, :] = (1.0 / step_size) * parts[c][FRONT:back]
            done[c, layer] = whole[c][FRONT:back]

    def scatter(layer):
        for c in range(3):
            start = (c * 16 + layer) * SPAN
            for row in range(start, start + SPAN):
                slots[pl.ds(slot_ref[row], 1), :] = rows[row : row + 1, :]

    copies = []
    for layer in range(18):
        second_step(layer)
        if layer >= 2:
            curl(layer - 2)
            scatter(layer - 2)
        if layer in (9, 17):
            part = len(copies)
            copies.append(
                pltpu.make_async_copy(
                    done.at[:, pl.ds(8 * part, 8)], next_ref.at[:, pl.ds(8 * part, 8)], sems.at[part]
                )
            )
            copies[part].start()
    out_ref[...] = slots[...].astype(jnp.bfloat16)
    for copy in copies:
        copy.wait()


def grid_update(target, low, high, right, base, squares, halves, keep, rate, slot):
    vmem = pl.BlockSpec(memory_space=pltpu.VMEM)
    return pl.pallas_call(
        grid_kernel,
        in_specs=[vmem] * 9 + [pl.BlockSpec(memory_space=pltpu.SMEM)],
        out_specs=[pl.BlockSpec(memory_space=pl.ANY), vmem],
        out_shape=[
            jax.ShapeDtypeStruct((3, 16, SPAN, EDGE), jnp.float32),
            jax.ShapeDtypeStruct((2 * slot.shape[0], EDGE), jnp.bfloat16),
        ],
        scratch_shapes=[
            pltpu.VMEM((2, 128, EDGE), jnp.float32),
            pltpu.VMEM((3, 20, WIDE, EDGE), jnp.float32),
            pltpu.VMEM((3, 20, WIDE, EDGE), jnp.float32),
            pltpu.VMEM((3, 18, WIDE, EDGE), jnp.float32),
            pltpu.VMEM((slot.shape[0], EDGE), jnp.float32),
            pltpu.VMEM((2 * slot.shape[0], EDGE), jnp.float32),
            pltpu.VMEM((3, 16, SPAN, EDGE), jnp.float32),
            pltpu.SemaphoreType.DMA((2,)),
        ],
        compiler_params=pltpu.CompilerParams(vmem_limit_bytes=24 * 1024 * 1024),
    )(target, low, high, right, base, squares, halves, keep, rate, slot)


def edges_kernel(sums_ref, left_ref, right_ref):
    for quarter in range(4):
        for k in range(2):
            row = 32 * quarter + 16 * k
            left_ref[row : row + 16, :] = sums_ref[16 * quarter + k, :, :EDGE]
            right_ref[row : row + 16, :] = sums_ref[16 * quarter + 14 + k, :, EDGE:]


def edges(sums):
    vmem = pl.BlockSpec(memory_space=pltpu.VMEM)
    return pl.pallas_call(
        edges_kernel,
        in_specs=[vmem],
        out_specs=[vmem] * 2,
        out_shape=[jax.ShapeDtypeStruct((128, EDGE), jnp.bfloat16)] * 2,
        compiler_params=pltpu.CompilerParams(vmem_limit_bytes=16 * 1024 * 1024),
    )(sums)


def chain(count):
    forward = [(i, i + 1) for i in range(count - 1)]
    return forward, [(target, source) for source, target in forward]


def slot_ranks(destination, block_count):
    count = destination.shape[0]
    one_hot = (destination[:, None] == jnp.arange(block_count, dtype=jnp.int32)[None, :]).astype(
        jnp.bfloat16
    )
    positions = jnp.arange(count, dtype=jnp.int32)
    lower = (positions[:, None] > positions[None, :]).astype(jnp.bfloat16)
    before = jnp.dot(lower, one_hot, preferred_element_type=jnp.float32)
    return jnp.sum(before * one_hot.astype(jnp.float32), axis=1).astype(jnp.int32)


def arrival_places(destination, places, receiver, capacity):
    count = destination.shape[1]
    to_me = destination == receiver
    positions = jnp.arange(count, dtype=jnp.int32)
    upper = (positions[:, None] < positions[None, :]).astype(jnp.bfloat16)
    rank = jnp.dot(
        to_me.astype(jnp.bfloat16), upper, preferred_element_type=jnp.float32
    ).astype(jnp.int32)
    rank = jnp.where(to_me, rank, -1)
    matches = rank[:, None, :] == jnp.arange(capacity, dtype=jnp.int32)[None, :, None]
    return jnp.sum(jnp.where(matches, places[:, None, :], 0), axis=2).reshape(-1)


def shards(
    velocity,
    stretch,
    coupling,
    strengths,
    remesh,
    green_left,
    green_right,
    tile_owner,
    tile_place,
    row_dest,
    row_place,
):
    blocks = lax.axis_size("blk")
    spans = lax.axis_size("span")
    my_block = lax.axis_index("blk")
    my_span = lax.axis_index("span")
    tile_count = remesh.shape[0] // EDGE
    grid_count = velocity.shape[0] * velocity.shape[1] * velocity.shape[2]
    row_cap = 2 * grid_count // blocks

    pieces = tile_pieces(remesh, strengths, green_left)
    held = (
        velocity,
        stretch,
        coupling,
        tile_owner,
        tile_place,
        row_dest,
        row_place,
    )
    pieces, held = lax.optimization_barrier((pieces, held))
    velocity, stretch, coupling, tile_owner, tile_place, row_dest, row_place = held
    arrived = lax.all_to_all(pieces, "blk", split_axis=0, concat_axis=0, tiled=True)

    def mine(values, count):
        rows = values.reshape(blocks, spans * count // EDGE, EDGE)
        if count >= EDGE:
            part = lax.dynamic_slice_in_dim(
                rows, my_span * (count // EDGE), count // EDGE, axis=1
            )
            return part.reshape(blocks, count)
        whole = rows.reshape(blocks, spans, count)
        return lax.dynamic_index_in_dim(whole, my_span, 1, keepdims=False)

    owners = mine(tile_owner.T, tile_count).reshape(1, -1)
    places = mine(tile_place, tile_count).reshape(1, -1)
    position = owners * 12 + places
    quarter = jnp.reshape(my_block // 16, (1,)).astype(jnp.int32)

    forward, backward = chain(spans)
    fields = (velocity, stretch, coupling[None])
    low = lax.ppermute(
        jnp.concatenate([f[:, :, -REACH:] for f in fields], axis=0), "span", forward
    )
    high = lax.ppermute(
        jnp.concatenate([f[:, :, :REACH] for f in fields], axis=0), "span", backward
    )

    destinations = mine(row_dest.T, grid_count)
    row_places = mine(row_place, grid_count)
    dest_mine = lax.dynamic_index_in_dim(destinations, my_block, 0, keepdims=False)
    row_slot = dest_mine * row_cap + slot_ranks(dest_mine, blocks)
    row_where = arrival_places(destinations, row_places, my_block, row_cap)
    remesh_rows = gathered_rows(row_where, remesh)
    low, high, position, row_slot, remesh_rows = lax.optimization_barrier(
        (low, high, position, row_slot, remesh_rows)
    )
    *extended, last, opening = widened(velocity, stretch, coupling, low, high)
    block_forward, block_backward = chain(blocks)
    low = lax.ppermute(last, "blk", block_forward)
    high = lax.ppermute(opening, "blk", block_backward)

    arrived, position, row_slot, remesh_rows = lax.optimization_barrier(
        (arrived, position, row_slot, remesh_rows)
    )
    sums = tile_sums(quarter, position, arrived.reshape(-1, 2 * EDGE))
    sums, extended, low, high = lax.optimization_barrier((sums, extended, low, high))
    sums = lax.all_to_all(
        sums.reshape(blocks, 16, 2 * EDGE), "blk", split_axis=0, concat_axis=0, tiled=True
    )
    left_edge, right_edge = edges(sums)
    target, base, squares, halves, keep, rate = fronted(
        sums.reshape(-1, 2 * EDGE), green_right, extended, low, high
    )
    low = lax.ppermute(right_edge, "span", forward)
    high = lax.ppermute(left_edge, "span", backward)
    current, outgoing = grid_update(
        target,
        low,
        high,
        green_right,
        base,
        squares,
        halves,
        keep,
        rate,
        row_slot,
    )
    incoming = lax.all_to_all(
        outgoing.reshape(blocks, row_cap, EDGE), "blk", split_axis=0, concat_axis=0, tiled=True
    )
    spread = lax.dot_general(
        remesh_rows,
        incoming.reshape(-1, EDGE),
        (((0,), (0,)), ((), ())),
        preferred_element_type=jnp.float32,
    )
    return current, (1.0 - blend) * strengths.astype(jnp.float32) + blend * spread


def solution(mesh):
    placed = (
        P(None, "blk", "span", None),
        P(None, "blk", "span", None),
        P("blk", "span", None),
        P(("blk", "span"), None),
        P(("blk", "span"), None),
        P(),
        P(),
        P(),
        P(),
        P(),
        P(),
    )
    return jax.shard_map(
        shards,
        mesh=mesh,
        in_specs=placed,
        out_specs=(P(None, "blk", "span", None), P(("blk", "span"), None)),
        check_vma=False,
    )
```

```python
import jax
import jax.numpy as jnp
from jax import lax
from jax.experimental import pallas as pl
from jax.experimental.pallas import tpu as pltpu
from jax.sharding import PartitionSpec as P

step_size = 0.05
viscosity = 0.4
blend = 0.5

EDGE = 128
REACH = 3
FRONT = 4
WIDE = 40
SLAB = 48
SPAN = 32
GROUP = 32
PITCH = GROUP + 1
ROW_PITCH = 17


def twice_diagonal(block):
    blank = jnp.zeros_like(block)
    return jnp.concatenate(
        [jnp.concatenate([block, blank], axis=1), jnp.concatenate([blank, block], axis=1)], axis=0
    )


def pieces_kernel(remesh_ref, strengths_ref, left_ref, out_ref, scratch):
    left = left_ref[...]
    strengths = twice_diagonal(strengths_ref[...])
    paired = jnp.concatenate(
        [
            jnp.concatenate(
                [remesh_ref[at : at + EDGE, :], remesh_ref[at + EDGE : at + 2 * EDGE, :]], axis=1
            )
            for at in range(0, GROUP * EDGE, 2 * EDGE)
        ],
        axis=0,
    )
    vortex = jnp.dot(paired, strengths, preferred_element_type=jnp.float32).astype(jnp.bfloat16)
    for pair in range(GROUP // 2):
        both = jnp.dot(
            left, vortex[pair * EDGE : (pair + 1) * EDGE], preferred_element_type=jnp.float32
        )
        for half in range(2):
            tile = 2 * pair + half
            for quarter in range(4):
                for side in range(2):
                    start = quarter * 32 + side * 16
                    scratch[
                        side, pl.ds(quarter * 16 * PITCH + tile, 16, stride=PITCH), :
                    ] = both[start : start + 16, half * EDGE : (half + 1) * EDGE]
    for side in range(2):
        for piece in range(64):
            out_ref[piece, :, side * EDGE : (side + 1) * EDGE] = scratch[
                side, piece * PITCH : piece * PITCH + GROUP, :
            ].astype(jnp.bfloat16)


def tile_pieces(remesh, strengths, left):
    tiles = remesh.shape[0] // EDGE
    return pl.pallas_call(
        pieces_kernel,
        grid=(tiles // GROUP,),
        in_specs=[
            pl.BlockSpec((GROUP * EDGE, EDGE), lambda g: (g, 0)),
            pl.BlockSpec((EDGE, EDGE), lambda g: (0, 0)),
            pl.BlockSpec((EDGE, EDGE), lambda g: (0, 0)),
        ],
        out_specs=pl.BlockSpec((64, GROUP, 2 * EDGE), lambda g: (0, g, 0)),
        out_shape=jax.ShapeDtypeStruct((64, tiles, 2 * EDGE), jnp.bfloat16),
        scratch_shapes=[pltpu.VMEM((2, 64 * PITCH, EDGE), jnp.float32)],
        compiler_params=pltpu.CompilerParams(vmem_limit_bytes=60 * 1024 * 1024),
    )(remesh, strengths, left)


def gather_kernel(index_ref, remesh_ref, out_ref, wide, picked):
    wide[...] = remesh_ref[...].astype(jnp.float32)

    def some(step, carry):
        for k in range(16):
            slot = step * 16 + k
            picked[pl.ds(slot, 1), :] = wide[pl.ds(index_ref[slot], 1), :]
        return carry

    lax.fori_loop(0, out_ref.shape[0] // 16, some, 0)
    out_ref[...] = picked[...].astype(jnp.bfloat16)


def gathered_rows(index, remesh):
    slots = index.shape[0]
    return pl.pallas_call(
        gather_kernel,
        in_specs=[
            pl.BlockSpec(memory_space=pltpu.SMEM),
            pl.BlockSpec(memory_space=pltpu.VMEM),
        ],
        out_specs=pl.BlockSpec(memory_space=pltpu.VMEM),
        out_shape=jax.ShapeDtypeStruct((slots, EDGE), jnp.bfloat16),
        scratch_shapes=[
            pltpu.VMEM(remesh.shape, jnp.float32),
            pltpu.VMEM((slots, EDGE), jnp.float32),
        ],
        compiler_params=pltpu.CompilerParams(vmem_limit_bytes=60 * 1024 * 1024),
        cost_estimate=pl.CostEstimate(flops=0, bytes_accessed=16 * 1024 * 1024, transcendentals=0),
    )(index, remesh)


def sums_kernel(quarter_ref, position_ref, arrived_ref, out_ref, spread):
    depth = 1024
    blocks = 64
    row = lax.broadcasted_iota(jnp.int32, (12 * blocks, EDGE), 0)
    wanted = (row % blocks) * 12 + row // blocks
    total = None
    for first in range(0, arrived_ref.shape[0], depth):
        picker = jnp.concatenate(
            [
                (wanted == position_ref[:, start : start + EDGE]).astype(jnp.bfloat16)
                for start in range(first, first + depth, EDGE)
            ],
            axis=1,
        )
        part = jnp.dot(
            picker, arrived_ref[first : first + depth, :], preferred_element_type=jnp.float32
        )
        total = part if total is None else total + part
    late = quarter_ref[0] >= 2
    block = lax.broadcasted_iota(jnp.int32, (blocks, EDGE), 0)
    for side in range(2):
        lanes = slice(side * EDGE, (side + 1) * EDGE)
        places = [total[p * blocks : (p + 1) * blocks, lanes] for p in range(12)]
        for component in range(3):
            before = pltpu.roll(places[component * 4 + 3], 1, 0)
            after = pltpu.roll(places[component * 4], blocks - 1, 0)
            places.append(
                jnp.where(
                    late,
                    jnp.where(block > 0, before, 0.0),
                    jnp.where(block < blocks - 1, after, 0.0),
                )
            )
        places.append(jnp.zeros((blocks, EDGE), jnp.float32))
        for entry, value in enumerate(places):
            spread[side, pl.ds(entry, blocks, stride=ROW_PITCH), :] = value
        for k in range(blocks):
            out_ref[16 * k : 16 * k + 16, lanes] = spread[
                side, ROW_PITCH * k : ROW_PITCH * k + 16, :
            ].astype(jnp.bfloat16)


def tile_sums(quarter, position, arrived):
    vmem = pl.BlockSpec(memory_space=pltpu.VMEM)
    return pl.pallas_call(
        sums_kernel,
        in_specs=[pl.BlockSpec(memory_space=pltpu.SMEM), vmem, vmem],
        out_specs=vmem,
        out_shape=jax.ShapeDtypeStruct((1024, 2 * EDGE), jnp.bfloat16),
        scratch_shapes=[pltpu.VMEM((2, 64 * ROW_PITCH, EDGE), jnp.float32)],
        compiler_params=pltpu.CompilerParams(vmem_limit_bytes=16 * 1024 * 1024),
    )(quarter, position, arrived)


def widen(out_ref, centre, low, high):
    out_ref[0:8, :] = jnp.zeros((8, EDGE), jnp.float32)
    out_ref[WIDE - 8 : WIDE, :] = jnp.zeros((8, EDGE), jnp.float32)
    out_ref[FRONT - REACH : FRONT, :] = low
    out_ref[FRONT + SPAN : FRONT + SPAN + REACH, :] = high
    out_ref[FRONT : FRONT + SPAN, :] = centre


def field_of(velocity_ref, stretch_ref, coupling_ref, f):
    if f < 3:
        return velocity_ref.at[f]
    return stretch_ref.at[f - 3] if f < 6 else coupling_ref


def slabs_kernel(
    velocity_ref, stretch_ref, coupling_ref, low_ref, high_ref, last_ref, first_ref, held
):
    blank = jnp.zeros((SLAB - WIDE, EDGE), jnp.float32)
    for f in range(7):
        field = field_of(velocity_ref, stretch_ref, coupling_ref, f)
        depth = 3 if f < 3 else 2
        at = 3 * f if f < 3 else 9 + 2 * (f - 3)
        for k in range(depth):
            for out_ref, layer in ((last_ref, 16 - depth + k), (first_ref, k)):
                one = held.at[0 if out_ref is last_ref else 1, at + k]
                widen(one, field[layer], low_ref[f, layer], high_ref[f, layer])
                out_ref[at + k] = jnp.concatenate([one[...], blank], axis=0).astype(jnp.bfloat16)


def slabs(velocity, stretch, coupling, low, high):
    vmem = pl.BlockSpec(memory_space=pltpu.VMEM)
    return pl.pallas_call(
        slabs_kernel,
        in_specs=[vmem] * 5,
        out_specs=[vmem] * 2,
        out_shape=[jax.ShapeDtypeStruct((17, SLAB, EDGE), jnp.bfloat16)] * 2,
        scratch_shapes=[pltpu.VMEM((2, 17, WIDE, EDGE), jnp.float32)],
        compiler_params=pltpu.CompilerParams(vmem_limit_bytes=16 * 1024 * 1024),
    )(velocity, stretch, coupling, low, high)


def unforced(source, at, squares, halves, keep, lanes):
    centre = [source[c, at] for c in range(3)]
    carried = [h * u for h, u in zip(halves, centre)]
    ahead_weight = [s - a for s, a in zip(squares, carried)]
    behind_weight = [s + a for s, a in zip(squares, carried)]
    ahead_weight[2] = jnp.where(lanes < EDGE - 1, ahead_weight[2], 0.0)
    behind_weight[2] = jnp.where(lanes > 0, behind_weight[2], 0.0)
    results = []
    for c in range(3):
        total = keep * centre[c]
        total = total + ahead_weight[0] * source[c, at + 1]
        total = total + behind_weight[0] * source[c, at - 1]
        total = total + ahead_weight[1] * pltpu.roll(centre[c], WIDE - 1, 0)
        total = total + behind_weight[1] * pltpu.roll(centre[c], 1, 0)
        total = total + ahead_weight[2] * pltpu.roll(centre[c], EDGE - 1, 1)
        total = total + behind_weight[2] * pltpu.roll(centre[c], 1, 1)
        results.append(total)
    return results


def entry_of(component, layer):
    chord = layer - 2
    entry = component * 4 + chord // 4 if 0 <= chord < 16 else 12 + component
    return chord % 4, entry


def slab_layer(ref, k):
    return ref[k].astype(jnp.float32)[:WIDE]


def front_kernel(
    sums_ref,
    right_ref,
    velocity_ref,
    stretch_ref,
    coupling_ref,
    span_low,
    span_high,
    low_ref,
    high_ref,
    target_ref,
    base_ref,
    squares_ref,
    halves_ref,
    keep_ref,
    rate_ref,
    velocity,
    metric,
    spread,
):
    blank = jnp.zeros((8, EDGE), jnp.float32)
    lanes = lax.broadcasted_iota(jnp.int32, (WIDE, EDGE), 1)
    product = jnp.dot(
        sums_ref[...], twice_diagonal(right_ref[...]), preferred_element_type=jnp.float32
    )
    for side in range(2):
        for piece in range(64):
            spread[side, piece * ROW_PITCH : piece * ROW_PITCH + 16, :] = product[
                piece * 16 : piece * 16 + 16, side * EDGE : (side + 1) * EDGE
            ]

    for c in range(3):
        for k in range(3):
            velocity[c, k] = slab_layer(low_ref, 3 * c + k)
            velocity[c, 19 + k] = slab_layer(high_ref, 3 * c + k)
    for f in range(7):
        field = field_of(velocity_ref, stretch_ref, coupling_ref, f)
        for layer in range(16):
            widen(
                velocity.at[f, layer + 3] if f < 3 else metric.at[f - 3, layer],
                field[layer],
                span_low[f, layer],
                span_high[f, layer],
            )

    for layer in range(20):
        inner = layer - 2
        if 0 <= inner < 16:
            stretch = [metric[d, inner] for d in range(3)]
            rate = metric[3, inner]
        else:
            slab, k = (low_ref, layer) if inner < 0 else (high_ref, inner - 16)
            stretch = [slab_layer(slab, 9 + 2 * d + k) for d in range(3)]
            rate = slab_layer(slab, 15 + k)
        squares = [(step_size * viscosity) * s * s for s in stretch]
        halves = [(0.5 * step_size) * s for s in stretch]
        keep = 1.0 - rate - 2.0 * (squares[0] + squares[1] + squares[2])
        results = unforced(velocity, layer + 1, squares, halves, keep, lanes)
        for d in range(3):
            squares_ref[d, layer] = squares[d]
            halves_ref[d, layer] = halves[d]
            base_ref[d, layer] = results[d]
        keep_ref[layer] = keep
        rate_ref[layer] = rate
        for component in range(3):
            quarter, entry = entry_of(component, layer)
            target_ref[component, layer, 0:8, :] = blank
            target_ref[component, layer, WIDE - 8 : WIDE, :] = blank
            for side in range(2):
                start = FRONT + 16 * side
                target_ref[component, layer, start : start + 16, :] = spread[
                    side, pl.ds(quarter * 16 * ROW_PITCH + entry, 16, stride=ROW_PITCH), :
                ]


def fronted(sums, right, fields, low, high):
    vmem = pl.BlockSpec(memory_space=pltpu.VMEM)
    return pl.pallas_call(
        front_kernel,
        in_specs=[vmem] * 9,
        out_specs=[vmem] * 6,
        out_shape=[jax.ShapeDtypeStruct((3, 20, WIDE, EDGE), jnp.float32)] * 4
        + [jax.ShapeDtypeStruct((20, WIDE, EDGE), jnp.float32)] * 2,
        scratch_shapes=[
            pltpu.VMEM((3, 22, WIDE, EDGE), jnp.float32),
            pltpu.VMEM((4, 16, WIDE, EDGE), jnp.float32),
            pltpu.VMEM((2, 64 * ROW_PITCH, EDGE), jnp.float32),
        ],
        compiler_params=pltpu.CompilerParams(vmem_limit_bytes=16 * 1024 * 1024),
        cost_estimate=pl.CostEstimate(
            flops=164 * 1000 * 1000, bytes_accessed=8 * 1024 * 1024, transcendentals=0
        ),
    )(sums, right, *fields, low, high)


def grid_kernel(
    target_ref,
    low_ref,
    high_ref,
    right_ref,
    base_ref,
    squares_ref,
    halves_ref,
    keep_ref,
    rate_ref,
    slot_ref,
    next_ref,
    out_ref,
    side_sums,
    forced,
    first,
    second,
    rows,
    slots,
    done,
    sems,
):
    right = right_ref[...]
    back = FRONT + SPAN
    lanes = lax.broadcasted_iota(jnp.int32, (WIDE, EDGE), 1)
    side_sums[0] = jnp.dot(low_ref[...], right, preferred_element_type=jnp.float32)
    side_sums[1] = jnp.dot(high_ref[...], right, preferred_element_type=jnp.float32)
    slots[...] = jnp.zeros_like(slots)
    for c in range(3):
        for layer in range(20):
            quarter, entry = entry_of(c, layer)
            forced[c, layer] = target_ref[c, layer]
            forced[c, layer, FRONT - 2 : FRONT, :] = side_sums[
                0, pl.ds(quarter * 32 + entry, 2, stride=16), :
            ]
            forced[c, layer, back : back + 2, :] = side_sums[
                1, pl.ds(quarter * 32 + entry, 2, stride=16), :
            ]
    for layer in range(20):
        rate = rate_ref[layer]
        for c in range(3):
            pull = rate * forced[c, layer]
            forced[c, layer] = pull
            first[c, layer] = base_ref[c, layer] + pull

    def second_step(layer):
        results = unforced(
            first,
            layer + 1,
            [squares_ref[d, layer + 1] for d in range(3)],
            [halves_ref[d, layer + 1] for d in range(3)],
            keep_ref[layer + 1],
            lanes,
        )
        for c in range(3):
            second[c, layer] = results[c] + forced[c, layer + 1]

    def curl(layer):
        whole = [second[c, layer + 1] for c in range(3)]
        half = [halves_ref[d, layer + 2] for d in range(3)]

        def slope(d, c):
            if d == 0:
                return half[0] * (second[c, layer + 2] - second[c, layer])
            if d == 1:
                ahead = pltpu.roll(whole[c], WIDE - 1, 0)
                behind = pltpu.roll(whole[c], 1, 0)
            else:
                ahead = jnp.where(lanes < EDGE - 1, pltpu.roll(whole[c], EDGE - 1, 1), 0.0)
                behind = jnp.where(lanes > 0, pltpu.roll(whole[c], 1, 1), 0.0)
            return half[d] * (ahead - behind)

        parts = (
            slope(1, 2) - slope(2, 1),
            slope(2, 0) - slope(0, 2),
            slope(0, 1) - slope(1, 0),
        )
        for c in range(3):
            start = (c * 16 + layer) * SPAN
            rows[start : start + SPAN, :] = (1.0 / step_size) * parts[c][FRONT:back]
            done[c, layer] = whole[c][FRONT:back]

    def scatter(layer):
        for c in range(3):
            start = (c * 16 + layer) * SPAN
            for row in range(start, start + SPAN):
                slots[pl.ds(slot_ref[row], 1), :] = rows[row : row + 1, :]

    copies = []
    for layer in range(18):
        second_step(layer)
        if layer >= 2:
            curl(layer - 2)
            scatter(layer - 2)
        if layer in (9, 17):
            part = len(copies)
            copies.append(
                pltpu.make_async_copy(
                    done.at[:, pl.ds(8 * part, 8)], next_ref.at[:, pl.ds(8 * part, 8)], sems.at[part]
                )
            )
            copies[part].start()
    out_ref[...] = slots[...].astype(jnp.bfloat16)
    for copy in copies:
        copy.wait()


def grid_update(target, low, high, right, base, squares, halves, keep, rate, slot):
    vmem = pl.BlockSpec(memory_space=pltpu.VMEM)
    return pl.pallas_call(
        grid_kernel,
        in_specs=[vmem] * 9 + [pl.BlockSpec(memory_space=pltpu.SMEM)],
        out_specs=[pl.BlockSpec(memory_space=pl.ANY), vmem],
        out_shape=[
            jax.ShapeDtypeStruct((3, 16, SPAN, EDGE), jnp.float32),
            jax.ShapeDtypeStruct((2 * slot.shape[0], EDGE), jnp.bfloat16),
        ],
        scratch_shapes=[
            pltpu.VMEM((2, 128, EDGE), jnp.float32),
            pltpu.VMEM((3, 20, WIDE, EDGE), jnp.float32),
            pltpu.VMEM((3, 20, WIDE, EDGE), jnp.float32),
            pltpu.VMEM((3, 18, WIDE, EDGE), jnp.float32),
            pltpu.VMEM((slot.shape[0], EDGE), jnp.float32),
            pltpu.VMEM((2 * slot.shape[0], EDGE), jnp.float32),
            pltpu.VMEM((3, 16, SPAN, EDGE), jnp.float32),
            pltpu.SemaphoreType.DMA((2,)),
        ],
        compiler_params=pltpu.CompilerParams(vmem_limit_bytes=24 * 1024 * 1024),
    )(target, low, high, right, base, squares, halves, keep, rate, slot)


def edges_kernel(sums_ref, left_ref, right_ref):
    for quarter in range(4):
        for k in range(2):
            row = 32 * quarter + 16 * k
            left_ref[row : row + 16, :] = sums_ref[16 * quarter + k, :, :EDGE]
            right_ref[row : row + 16, :] = sums_ref[16 * quarter + 14 + k, :, EDGE:]


def edges(sums):
    vmem = pl.BlockSpec(memory_space=pltpu.VMEM)
    return pl.pallas_call(
        edges_kernel,
        in_specs=[vmem],
        out_specs=[vmem] * 2,
        out_shape=[jax.ShapeDtypeStruct((128, EDGE), jnp.bfloat16)] * 2,
        compiler_params=pltpu.CompilerParams(vmem_limit_bytes=16 * 1024 * 1024),
    )(sums)


def chain(count):
    forward = [(i, i + 1) for i in range(count - 1)]
    return forward, [(target, source) for source, target in forward]


def slot_ranks(destination, block_count):
    count = destination.shape[0]
    one_hot = (destination[:, None] == jnp.arange(block_count, dtype=jnp.int32)[None, :]).astype(
        jnp.bfloat16
    )
    positions = jnp.arange(count, dtype=jnp.int32)
    lower = (positions[:, None] > positions[None, :]).astype(jnp.bfloat16)
    before = jnp.dot(lower, one_hot, preferred_element_type=jnp.float32)
    return jnp.sum(before * one_hot.astype(jnp.float32), axis=1).astype(jnp.int32)


def arrival_places(destination, places, receiver, capacity):
    count = destination.shape[1]
    to_me = destination == receiver
    positions = jnp.arange(count, dtype=jnp.int32)
    upper = (positions[:, None] < positions[None, :]).astype(jnp.bfloat16)
    rank = jnp.dot(
        to_me.astype(jnp.bfloat16), upper, preferred_element_type=jnp.float32
    ).astype(jnp.int32)
    rank = jnp.where(to_me, rank, -1)
    matches = rank[:, None, :] == jnp.arange(capacity, dtype=jnp.int32)[None, :, None]
    return jnp.sum(jnp.where(matches, places[:, None, :], 0), axis=2).reshape(-1)


def shards(
    velocity,
    stretch,
    coupling,
    strengths,
    remesh,
    green_left,
    green_right,
    tile_owner,
    tile_place,
    row_dest,
    row_place,
):
    blocks = lax.axis_size("blk")
    spans = lax.axis_size("span")
    my_block = lax.axis_index("blk")
    my_span = lax.axis_index("span")
    tile_count = remesh.shape[0] // EDGE
    grid_count = velocity.shape[0] * velocity.shape[1] * velocity.shape[2]
    row_cap = 2 * grid_count // blocks

    pieces = tile_pieces(remesh, strengths, green_left)
    held = (
        velocity,
        stretch,
        coupling,
        tile_owner,
        tile_place,
        row_dest,
        row_place,
    )
    pieces, held = lax.optimization_barrier((pieces, held))
    velocity, stretch, coupling, tile_owner, tile_place, row_dest, row_place = held
    arrived = lax.all_to_all(pieces, "blk", split_axis=0, concat_axis=0, tiled=True)

    def mine(values, count):
        rows = values.reshape(blocks, spans * count // EDGE, EDGE)
        if count >= EDGE:
            part = lax.dynamic_slice_in_dim(
                rows, my_span * (count // EDGE), count // EDGE, axis=1
            )
            return part.reshape(blocks, count)
        whole = rows.reshape(blocks, spans, count)
        return lax.dynamic_index_in_dim(whole, my_span, 1, keepdims=False)

    owners = mine(tile_owner.T, tile_count).reshape(1, -1)
    places = mine(tile_place, tile_count).reshape(1, -1)
    position = owners * 12 + places
    quarter = jnp.reshape(my_block // 16, (1,)).astype(jnp.int32)

    forward, backward = chain(spans)
    fields = (velocity, stretch, coupling[None])
    low = lax.ppermute(
        jnp.concatenate([f[:, :, -REACH:] for f in fields], axis=0), "span", forward
    )
    high = lax.ppermute(
        jnp.concatenate([f[:, :, :REACH] for f in fields], axis=0), "span", backward
    )

    last, opening = slabs(velocity, stretch, coupling, low, high)
    extended = (velocity, stretch, coupling, low, high)
    block_forward, block_backward = chain(blocks)
    low = lax.ppermute(last, "blk", block_forward)
    high = lax.ppermute(opening, "blk", block_backward)

    destinations = mine(row_dest.T, grid_count)
    row_places = mine(row_place, grid_count)
    dest_mine = lax.dynamic_index_in_dim(destinations, my_block, 0, keepdims=False)
    row_slot = dest_mine * row_cap + slot_ranks(dest_mine, blocks)
    row_where = arrival_places(destinations, row_places, my_block, row_cap)
    remesh_rows = gathered_rows(row_where, remesh)

    arrived, position, row_slot, remesh_rows = lax.optimization_barrier(
        (arrived, position, row_slot, remesh_rows)
    )
    sums = tile_sums(quarter, position, arrived.reshape(-1, 2 * EDGE))
    sums, extended, low, high = lax.optimization_barrier((sums, extended, low, high))
    sums = lax.all_to_all(
        sums.reshape(blocks, 16, 2 * EDGE), "blk", split_axis=0, concat_axis=0, tiled=True
    )
    left_edge, right_edge = edges(sums)
    target, base, squares, halves, keep, rate = fronted(
        sums.reshape(-1, 2 * EDGE), green_right, extended, low, high
    )
    low = lax.ppermute(right_edge, "span", forward)
    high = lax.ppermute(left_edge, "span", backward)
    current, outgoing = grid_update(
        target,
        low,
        high,
        green_right,
        base,
        squares,
        halves,
        keep,
        rate,
        row_slot,
    )
    incoming = lax.all_to_all(
        outgoing.reshape(blocks, row_cap, EDGE), "blk", split_axis=0, concat_axis=0, tiled=True
    )
    spread = lax.dot_general(
        remesh_rows,
        incoming.reshape(-1, EDGE),
        (((0,), (0,)), ((), ())),
        preferred_element_type=jnp.float32,
    )
    return current, (1.0 - blend) * strengths.astype(jnp.float32) + blend * spread


def solution(mesh):
    placed = (
        P(None, "blk", "span", None),
        P(None, "blk", "span", None),
        P("blk", "span", None),
        P(("blk", "span"), None),
        P(("blk", "span"), None),
        P(),
        P(),
        P(),
        P(),
        P(),
        P(),
    )
    return jax.shard_map(
        shards,
        mesh=mesh,
        in_specs=placed,
        out_specs=(P(None, "blk", "span", None), P(("blk", "span"), None)),
        check_vma=False,
    )
```

```python
import jax
import jax.numpy as jnp
from jax import lax
from jax.experimental import pallas as pl
from jax.experimental.pallas import tpu as pltpu
from jax.sharding import PartitionSpec as P

step_size = 0.05
viscosity = 0.4
blend = 0.5

EDGE = 128
REACH = 3
FRONT = 4
WIDE = 40
SLAB = 48
SPAN = 32
GROUP = 32
PITCH = GROUP + 1
ROW_PITCH = 17


def twice_diagonal(block):
    blank = jnp.zeros_like(block)
    return jnp.concatenate(
        [jnp.concatenate([block, blank], axis=1), jnp.concatenate([blank, block], axis=1)], axis=0
    )


def pieces_kernel(remesh_ref, strengths_ref, left_ref, out_ref, scratch):
    left = left_ref[...]
    strengths = twice_diagonal(strengths_ref[...])
    paired = jnp.concatenate(
        [
            jnp.concatenate(
                [remesh_ref[at : at + EDGE, :], remesh_ref[at + EDGE : at + 2 * EDGE, :]], axis=1
            )
            for at in range(0, GROUP * EDGE, 2 * EDGE)
        ],
        axis=0,
    )
    vortex = jnp.dot(paired, strengths, preferred_element_type=jnp.float32).astype(jnp.bfloat16)
    for pair in range(GROUP // 2):
        both = jnp.dot(
            left, vortex[pair * EDGE : (pair + 1) * EDGE], preferred_element_type=jnp.float32
        )
        for half in range(2):
            tile = 2 * pair + half
            for quarter in range(4):
                for side in range(2):
                    start = quarter * 32 + side * 16
                    scratch[
                        side, pl.ds(quarter * 16 * PITCH + tile, 16, stride=PITCH), :
                    ] = both[start : start + 16, half * EDGE : (half + 1) * EDGE]
    for side in range(2):
        for piece in range(64):
            out_ref[piece, :, side * EDGE : (side + 1) * EDGE] = scratch[
                side, piece * PITCH : piece * PITCH + GROUP, :
            ].astype(jnp.bfloat16)


def tile_pieces(remesh, strengths, left):
    tiles = remesh.shape[0] // EDGE
    return pl.pallas_call(
        pieces_kernel,
        grid=(tiles // GROUP,),
        in_specs=[
            pl.BlockSpec((GROUP * EDGE, EDGE), lambda g: (g, 0)),
            pl.BlockSpec((EDGE, EDGE), lambda g: (0, 0)),
            pl.BlockSpec((EDGE, EDGE), lambda g: (0, 0)),
        ],
        out_specs=pl.BlockSpec((64, GROUP, 2 * EDGE), lambda g: (0, g, 0)),
        out_shape=jax.ShapeDtypeStruct((64, tiles, 2 * EDGE), jnp.bfloat16),
        scratch_shapes=[pltpu.VMEM((2, 65 * PITCH, EDGE), jnp.float32)],
        compiler_params=pltpu.CompilerParams(vmem_limit_bytes=60 * 1024 * 1024),
    )(remesh, strengths, left)


def gather_kernel(index_ref, remesh_ref, out_ref, wide, picked):
    wide[...] = remesh_ref[...].astype(jnp.float32)

    def some(step, carry):
        for k in range(16):
            slot = step * 16 + k
            picked[pl.ds(slot, 1), :] = wide[pl.ds(index_ref[slot], 1), :]
        return carry

    lax.fori_loop(0, out_ref.shape[0] // 16, some, 0)
    out_ref[...] = picked[...].astype(jnp.bfloat16)


def gathered_rows(index, remesh):
    slots = index.shape[0]
    return pl.pallas_call(
        gather_kernel,
        in_specs=[
            pl.BlockSpec(memory_space=pltpu.SMEM),
            pl.BlockSpec(memory_space=pltpu.VMEM),
        ],
        out_specs=pl.BlockSpec(memory_space=pltpu.VMEM),
        out_shape=jax.ShapeDtypeStruct((slots, EDGE), jnp.bfloat16),
        scratch_shapes=[
            pltpu.VMEM(remesh.shape, jnp.float32),
            pltpu.VMEM((slots, EDGE), jnp.float32),
        ],
        compiler_params=pltpu.CompilerParams(vmem_limit_bytes=60 * 1024 * 1024),
        cost_estimate=pl.CostEstimate(flops=0, bytes_accessed=16 * 1024 * 1024, transcendentals=0),
    )(index, remesh)


def sums_kernel(quarter_ref, position_ref, arrived_ref, out_ref, spread):
    depth = 1024
    blocks = 64
    row = lax.broadcasted_iota(jnp.int32, (12 * blocks, EDGE), 0)
    wanted = (row % blocks) * 12 + row // blocks
    total = None
    for first in range(0, arrived_ref.shape[0], depth):
        picker = jnp.concatenate(
            [
                (wanted == position_ref[:, start : start + EDGE]).astype(jnp.bfloat16)
                for start in range(first, first + depth, EDGE)
            ],
            axis=1,
        )
        part = jnp.dot(
            picker, arrived_ref[first : first + depth, :], preferred_element_type=jnp.float32
        )
        total = part if total is None else total + part
    late = quarter_ref[0] >= 2
    block = lax.broadcasted_iota(jnp.int32, (blocks, EDGE), 0)
    for side in range(2):
        lanes = slice(side * EDGE, (side + 1) * EDGE)
        places = [total[p * blocks : (p + 1) * blocks, lanes] for p in range(12)]
        for component in range(3):
            before = pltpu.roll(places[component * 4 + 3], 1, 0)
            after = pltpu.roll(places[component * 4], blocks - 1, 0)
            places.append(
                jnp.where(
                    late,
                    jnp.where(block > 0, before, 0.0),
                    jnp.where(block < blocks - 1, after, 0.0),
                )
            )
        places.append(jnp.zeros((blocks, EDGE), jnp.float32))
        for entry, value in enumerate(places):
            spread[side, pl.ds(entry, blocks, stride=ROW_PITCH), :] = value
        for k in range(blocks):
            out_ref[16 * k : 16 * k + 16, lanes] = spread[
                side, ROW_PITCH * k : ROW_PITCH * k + 16, :
            ].astype(jnp.bfloat16)


def tile_sums(quarter, position, arrived):
    vmem = pl.BlockSpec(memory_space=pltpu.VMEM)
    return pl.pallas_call(
        sums_kernel,
        in_specs=[pl.BlockSpec(memory_space=pltpu.SMEM), vmem, vmem],
        out_specs=vmem,
        out_shape=jax.ShapeDtypeStruct((1024, 2 * EDGE), jnp.bfloat16),
        scratch_shapes=[pltpu.VMEM((2, 65 * ROW_PITCH, EDGE), jnp.float32)],
        compiler_params=pltpu.CompilerParams(vmem_limit_bytes=16 * 1024 * 1024),
    )(quarter, position, arrived)


def widen(out_ref, centre, low, high):
    out_ref[0:8, :] = jnp.zeros((8, EDGE), jnp.float32)
    out_ref[WIDE - 8 : WIDE, :] = jnp.zeros((8, EDGE), jnp.float32)
    out_ref[FRONT - REACH : FRONT, :] = low
    out_ref[FRONT + SPAN : FRONT + SPAN + REACH, :] = high
    out_ref[FRONT : FRONT + SPAN, :] = centre


def field_of(velocity_ref, stretch_ref, coupling_ref, f):
    if f < 3:
        return velocity_ref.at[f]
    return stretch_ref.at[f - 3] if f < 6 else coupling_ref


def slabs_kernel(
    velocity_ref, stretch_ref, coupling_ref, low_ref, high_ref, last_ref, first_ref, held
):
    blank = jnp.zeros((SLAB - WIDE, EDGE), jnp.float32)
    for f in range(7):
        field = field_of(velocity_ref, stretch_ref, coupling_ref, f)
        depth = 3 if f < 3 else 2
        at = 3 * f if f < 3 else 9 + 2 * (f - 3)
        for k in range(depth):
            for out_ref, layer in ((last_ref, 16 - depth + k), (first_ref, k)):
                one = held.at[0 if out_ref is last_ref else 1, at + k]
                widen(one, field[layer], low_ref[f, layer], high_ref[f, layer])
                out_ref[at + k] = jnp.concatenate([one[...], blank], axis=0).astype(jnp.bfloat16)


def slabs(velocity, stretch, coupling, low, high):
    vmem = pl.BlockSpec(memory_space=pltpu.VMEM)
    return pl.pallas_call(
        slabs_kernel,
        in_specs=[vmem] * 5,
        out_specs=[vmem] * 2,
        out_shape=[jax.ShapeDtypeStruct((17, SLAB, EDGE), jnp.bfloat16)] * 2,
        scratch_shapes=[pltpu.VMEM((2, 17, WIDE, EDGE), jnp.float32)],
        compiler_params=pltpu.CompilerParams(vmem_limit_bytes=16 * 1024 * 1024),
    )(velocity, stretch, coupling, low, high)


def unforced(source, at, squares, halves, keep, lanes):
    centre = [source[c, at] for c in range(3)]
    carried = [h * u for h, u in zip(halves, centre)]
    ahead_weight = [s - a for s, a in zip(squares, carried)]
    behind_weight = [s + a for s, a in zip(squares, carried)]
    ahead_weight[2] = jnp.where(lanes < EDGE - 1, ahead_weight[2], 0.0)
    behind_weight[2] = jnp.where(lanes > 0, behind_weight[2], 0.0)
    results = []
    for c in range(3):
        total = keep * centre[c]
        total = total + ahead_weight[0] * source[c, at + 1]
        total = total + behind_weight[0] * source[c, at - 1]
        total = total + ahead_weight[1] * pltpu.roll(centre[c], WIDE - 1, 0)
        total = total + behind_weight[1] * pltpu.roll(centre[c], 1, 0)
        total = total + ahead_weight[2] * pltpu.roll(centre[c], EDGE - 1, 1)
        total = total + behind_weight[2] * pltpu.roll(centre[c], 1, 1)
        results.append(total)
    return results


def entry_of(component, layer):
    chord = layer - 2
    entry = component * 4 + chord // 4 if 0 <= chord < 16 else 12 + component
    return chord % 4, entry


def slab_layer(ref, k):
    return ref[k].astype(jnp.float32)[:WIDE]


def front_kernel(
    sums_ref,
    right_ref,
    velocity_ref,
    stretch_ref,
    coupling_ref,
    span_low,
    span_high,
    low_ref,
    high_ref,
    target_ref,
    base_ref,
    squares_ref,
    halves_ref,
    keep_ref,
    rate_ref,
    velocity,
    metric,
    spread,
):
    blank = jnp.zeros((8, EDGE), jnp.float32)
    lanes = lax.broadcasted_iota(jnp.int32, (WIDE, EDGE), 1)
    product = jnp.dot(
        sums_ref[...], twice_diagonal(right_ref[...]), preferred_element_type=jnp.float32
    )
    for side in range(2):
        for piece in range(64):
            spread[side, piece * ROW_PITCH : piece * ROW_PITCH + 16, :] = product[
                piece * 16 : piece * 16 + 16, side * EDGE : (side + 1) * EDGE
            ]

    for c in range(3):
        for k in range(3):
            velocity[c, k] = slab_layer(low_ref, 3 * c + k)
            velocity[c, 19 + k] = slab_layer(high_ref, 3 * c + k)
    for f in range(7):
        field = field_of(velocity_ref, stretch_ref, coupling_ref, f)
        for layer in range(16):
            widen(
                velocity.at[f, layer + 3] if f < 3 else metric.at[f - 3, layer],
                field[layer],
                span_low[f, layer],
                span_high[f, layer],
            )

    for layer in range(20):
        inner = layer - 2
        if 0 <= inner < 16:
            stretch = [metric[d, inner] for d in range(3)]
            rate = metric[3, inner]
        else:
            slab, k = (low_ref, layer) if inner < 0 else (high_ref, inner - 16)
            stretch = [slab_layer(slab, 9 + 2 * d + k) for d in range(3)]
            rate = slab_layer(slab, 15 + k)
        squares = [(step_size * viscosity) * s * s for s in stretch]
        halves = [(0.5 * step_size) * s for s in stretch]
        keep = 1.0 - rate - 2.0 * (squares[0] + squares[1] + squares[2])
        results = unforced(velocity, layer + 1, squares, halves, keep, lanes)
        for d in range(3):
            squares_ref[d, layer] = squares[d]
            halves_ref[d, layer] = halves[d]
            base_ref[d, layer] = results[d]
        keep_ref[layer] = keep
        rate_ref[layer] = rate
        for component in range(3):
            quarter, entry = entry_of(component, layer)
            target_ref[component, layer, 0:8, :] = blank
            target_ref[component, layer, WIDE - 8 : WIDE, :] = blank
            for side in range(2):
                start = FRONT + 16 * side
                target_ref[component, layer, start : start + 16, :] = spread[
                    side, pl.ds(quarter * 16 * ROW_PITCH + entry, 16, stride=ROW_PITCH), :
                ]


def fronted(sums, right, fields, low, high):
    vmem = pl.BlockSpec(memory_space=pltpu.VMEM)
    return pl.pallas_call(
        front_kernel,
        in_specs=[vmem] * 9,
        out_specs=[vmem] * 6,
        out_shape=[jax.ShapeDtypeStruct((3, 20, WIDE, EDGE), jnp.float32)] * 4
        + [jax.ShapeDtypeStruct((20, WIDE, EDGE), jnp.float32)] * 2,
        scratch_shapes=[
            pltpu.VMEM((3, 22, WIDE, EDGE), jnp.float32),
            pltpu.VMEM((4, 16, WIDE, EDGE), jnp.float32),
            pltpu.VMEM((2, 65 * ROW_PITCH, EDGE), jnp.float32),
        ],
        compiler_params=pltpu.CompilerParams(vmem_limit_bytes=16 * 1024 * 1024),
        cost_estimate=pl.CostEstimate(
            flops=164 * 1000 * 1000, bytes_accessed=8 * 1024 * 1024, transcendentals=0
        ),
    )(sums, right, *fields, low, high)


def grid_kernel(
    target_ref,
    low_ref,
    high_ref,
    right_ref,
    base_ref,
    squares_ref,
    halves_ref,
    keep_ref,
    rate_ref,
    slot_ref,
    next_ref,
    out_ref,
    side_sums,
    forced,
    first,
    second,
    rows,
    slots,
    done,
    sems,
):
    right = right_ref[...]
    back = FRONT + SPAN
    lanes = lax.broadcasted_iota(jnp.int32, (WIDE, EDGE), 1)
    for side, ref in enumerate((low_ref, high_ref)):
        side_sums[side, 0:128, :] = jnp.dot(ref[...], right, preferred_element_type=jnp.float32)
    slots[...] = jnp.zeros_like(slots)
    for c in range(3):
        for layer in range(20):
            quarter, entry = entry_of(c, layer)
            forced[c, layer] = target_ref[c, layer]
            forced[c, layer, FRONT - 2 : FRONT, :] = side_sums[
                0, pl.ds(quarter * 32 + entry, 2, stride=16), :
            ]
            forced[c, layer, back : back + 2, :] = side_sums[
                1, pl.ds(quarter * 32 + entry, 2, stride=16), :
            ]
    for layer in range(20):
        rate = rate_ref[layer]
        for c in range(3):
            pull = rate * forced[c, layer]
            forced[c, layer] = pull
            first[c, layer] = base_ref[c, layer] + pull

    def second_step(layer):
        results = unforced(
            first,
            layer + 1,
            [squares_ref[d, layer + 1] for d in range(3)],
            [halves_ref[d, layer + 1] for d in range(3)],
            keep_ref[layer + 1],
            lanes,
        )
        for c in range(3):
            second[c, layer] = results[c] + forced[c, layer + 1]

    def curl(layer):
        whole = [second[c, layer + 1] for c in range(3)]
        half = [halves_ref[d, layer + 2] for d in range(3)]

        def slope(d, c):
            if d == 0:
                return half[0] * (second[c, layer + 2] - second[c, layer])
            if d == 1:
                ahead = pltpu.roll(whole[c], WIDE - 1, 0)
                behind = pltpu.roll(whole[c], 1, 0)
            else:
                ahead = jnp.where(lanes < EDGE - 1, pltpu.roll(whole[c], EDGE - 1, 1), 0.0)
                behind = jnp.where(lanes > 0, pltpu.roll(whole[c], 1, 1), 0.0)
            return half[d] * (ahead - behind)

        parts = (
            slope(1, 2) - slope(2, 1),
            slope(2, 0) - slope(0, 2),
            slope(0, 1) - slope(1, 0),
        )
        for c in range(3):
            start = (c * 16 + layer) * SPAN
            rows[start : start + SPAN, :] = (1.0 / step_size) * parts[c][FRONT:back]
            done[c, layer] = whole[c][FRONT:back]

    def scatter(layer):
        for c in range(3):
            start = (c * 16 + layer) * SPAN
            for row in range(start, start + SPAN):
                slots[pl.ds(slot_ref[row], 1), :] = rows[row : row + 1, :]

    copies = []
    for layer in range(18):
        second_step(layer)
        if layer >= 2:
            curl(layer - 2)
            scatter(layer - 2)
        if layer in (9, 17):
            part = len(copies)
            copies.append(
                pltpu.make_async_copy(
                    done.at[:, pl.ds(8 * part, 8)], next_ref.at[:, pl.ds(8 * part, 8)], sems.at[part]
                )
            )
            copies[part].start()
    out_ref[...] = slots[...].astype(jnp.bfloat16)
    for copy in copies:
        copy.wait()


def grid_update(target, low, high, right, base, squares, halves, keep, rate, slot):
    vmem = pl.BlockSpec(memory_space=pltpu.VMEM)
    return pl.pallas_call(
        grid_kernel,
        in_specs=[vmem] * 9 + [pl.BlockSpec(memory_space=pltpu.SMEM)],
        out_specs=[pl.BlockSpec(memory_space=pl.ANY), vmem],
        out_shape=[
            jax.ShapeDtypeStruct((3, 16, SPAN, EDGE), jnp.float32),
            jax.ShapeDtypeStruct((2 * slot.shape[0], EDGE), jnp.bfloat16),
        ],
        scratch_shapes=[
            pltpu.VMEM((2, 144, EDGE), jnp.float32),
            pltpu.VMEM((3, 20, WIDE, EDGE), jnp.float32),
            pltpu.VMEM((3, 20, WIDE, EDGE), jnp.float32),
            pltpu.VMEM((3, 18, WIDE, EDGE), jnp.float32),
            pltpu.VMEM((slot.shape[0], EDGE), jnp.float32),
            pltpu.VMEM((2 * slot.shape[0], EDGE), jnp.float32),
            pltpu.VMEM((3, 16, SPAN, EDGE), jnp.float32),
            pltpu.SemaphoreType.DMA((2,)),
        ],
        compiler_params=pltpu.CompilerParams(vmem_limit_bytes=24 * 1024 * 1024),
    )(target, low, high, right, base, squares, halves, keep, rate, slot)


def edges_kernel(sums_ref, left_ref, right_ref):
    for quarter in range(4):
        for k in range(2):
            row = 32 * quarter + 16 * k
            left_ref[row : row + 16, :] = sums_ref[16 * quarter + k, :, :EDGE]
            right_ref[row : row + 16, :] = sums_ref[16 * quarter + 14 + k, :, EDGE:]


def edges(sums):
    vmem = pl.BlockSpec(memory_space=pltpu.VMEM)
    return pl.pallas_call(
        edges_kernel,
        in_specs=[vmem],
        out_specs=[vmem] * 2,
        out_shape=[jax.ShapeDtypeStruct((128, EDGE), jnp.bfloat16)] * 2,
        compiler_params=pltpu.CompilerParams(vmem_limit_bytes=16 * 1024 * 1024),
    )(sums)


def chain(count):
    forward = [(i, i + 1) for i in range(count - 1)]
    return forward, [(target, source) for source, target in forward]


def slot_ranks(destination, block_count):
    count = destination.shape[0]
    one_hot = (destination[:, None] == jnp.arange(block_count, dtype=jnp.int32)[None, :]).astype(
        jnp.bfloat16
    )
    positions = jnp.arange(count, dtype=jnp.int32)
    lower = (positions[:, None] > positions[None, :]).astype(jnp.bfloat16)
    before = jnp.dot(lower, one_hot, preferred_element_type=jnp.float32)
    return jnp.sum(before * one_hot.astype(jnp.float32), axis=1).astype(jnp.int32)


def arrival_places(destination, places, receiver, capacity):
    count = destination.shape[1]
    to_me = destination == receiver
    positions = jnp.arange(count, dtype=jnp.int32)
    upper = (positions[:, None] < positions[None, :]).astype(jnp.bfloat16)
    rank = jnp.dot(
        to_me.astype(jnp.bfloat16), upper, preferred_element_type=jnp.float32
    ).astype(jnp.int32)
    rank = jnp.where(to_me, rank, -1)
    matches = rank[:, None, :] == jnp.arange(capacity, dtype=jnp.int32)[None, :, None]
    return jnp.sum(jnp.where(matches, places[:, None, :], 0), axis=2).reshape(-1)


def shards(
    velocity,
    stretch,
    coupling,
    strengths,
    remesh,
    green_left,
    green_right,
    tile_owner,
    tile_place,
    row_dest,
    row_place,
):
    blocks = lax.axis_size("blk")
    spans = lax.axis_size("span")
    my_block = lax.axis_index("blk")
    my_span = lax.axis_index("span")
    tile_count = remesh.shape[0] // EDGE
    grid_count = velocity.shape[0] * velocity.shape[1] * velocity.shape[2]
    row_cap = 2 * grid_count // blocks

    pieces = tile_pieces(remesh, strengths, green_left)
    held = (
        velocity,
        stretch,
        coupling,
        tile_owner,
        tile_place,
        row_dest,
        row_place,
    )
    pieces, held = lax.optimization_barrier((pieces, held))
    velocity, stretch, coupling, tile_owner, tile_place, row_dest, row_place = held
    arrived = lax.all_to_all(pieces, "blk", split_axis=0, concat_axis=0, tiled=True)

    def mine(values, count):
        rows = values.reshape(blocks, spans * count // EDGE, EDGE)
        if count >= EDGE:
            part = lax.dynamic_slice_in_dim(
                rows, my_span * (count // EDGE), count // EDGE, axis=1
            )
            return part.reshape(blocks, count)
        whole = rows.reshape(blocks, spans, count)
        return lax.dynamic_index_in_dim(whole, my_span, 1, keepdims=False)

    owners = mine(tile_owner.T, tile_count).reshape(1, -1)
    places = mine(tile_place, tile_count).reshape(1, -1)
    position = owners * 12 + places
    quarter = jnp.reshape(my_block // 16, (1,)).astype(jnp.int32)

    forward, backward = chain(spans)
    fields = (velocity, stretch, coupling[None])
    low = lax.ppermute(
        jnp.concatenate([f[:, :, -REACH:] for f in fields], axis=0), "span", forward
    )
    high = lax.ppermute(
        jnp.concatenate([f[:, :, :REACH] for f in fields], axis=0), "span", backward
    )

    last, opening = slabs(velocity, stretch, coupling, low, high)
    extended = (velocity, stretch, coupling, low, high)
    block_forward, block_backward = chain(blocks)
    low = lax.ppermute(last, "blk", block_forward)
    high = lax.ppermute(opening, "blk", block_backward)

    destinations = mine(row_dest.T, grid_count)
    row_places = mine(row_place, grid_count)
    dest_mine = lax.dynamic_index_in_dim(destinations, my_block, 0, keepdims=False)
    row_slot = dest_mine * row_cap + slot_ranks(dest_mine, blocks)
    row_where = arrival_places(destinations, row_places, my_block, row_cap)
    remesh_rows = gathered_rows(row_where, remesh)

    arrived, position, row_slot, remesh_rows = lax.optimization_barrier(
        (arrived, position, row_slot, remesh_rows)
    )
    sums = tile_sums(quarter, position, arrived.reshape(-1, 2 * EDGE))
    sums, extended, low, high = lax.optimization_barrier((sums, extended, low, high))
    sums = lax.all_to_all(
        sums.reshape(blocks, 16, 2 * EDGE), "blk", split_axis=0, concat_axis=0, tiled=True
    )
    left_edge, right_edge = edges(sums)
    target, base, squares, halves, keep, rate = fronted(
        sums.reshape(-1, 2 * EDGE), green_right, extended, low, high
    )
    low = lax.ppermute(right_edge, "span", forward)
    high = lax.ppermute(left_edge, "span", backward)
    current, outgoing = grid_update(
        target,
        low,
        high,
        green_right,
        base,
        squares,
        halves,
        keep,
        rate,
        row_slot,
    )
    incoming = lax.all_to_all(
        outgoing.reshape(blocks, row_cap, EDGE), "blk", split_axis=0, concat_axis=0, tiled=True
    )
    spread = lax.dot_general(
        remesh_rows,
        incoming.reshape(-1, EDGE),
        (((0,), (0,)), ((), ())),
        preferred_element_type=jnp.float32,
    )
    return current, (1.0 - blend) * strengths.astype(jnp.float32) + blend * spread


def solution(mesh):
    placed = (
        P(None, "blk", "span", None),
        P(None, "blk", "span", None),
        P("blk", "span", None),
        P(("blk", "span"), None),
        P(("blk", "span"), None),
        P(),
        P(),
        P(),
        P(),
        P(),
        P(),
    )
    return jax.shard_map(
        shards,
        mesh=mesh,
        in_specs=placed,
        out_specs=(P(None, "blk", "span", None), P(("blk", "span"), None)),
        check_vma=False,
    )
```

```python
import jax
import jax.numpy as jnp
from jax import lax
from jax.experimental import pallas as pl
from jax.experimental.pallas import tpu as pltpu
from jax.sharding import PartitionSpec as P

step_size = 0.05
viscosity = 0.4
blend = 0.5

EDGE = 128
REACH = 3
FRONT = 4
WIDE = 40
SLAB = 48
SPAN = 32
GROUP = 32
PITCH = GROUP + 1
ROW_PITCH = 17


def twice_diagonal(block):
    blank = jnp.zeros_like(block)
    return jnp.concatenate(
        [jnp.concatenate([block, blank], axis=1), jnp.concatenate([blank, block], axis=1)], axis=0
    )


def pieces_kernel(remesh_ref, strengths_ref, left_ref, out_ref, scratch):
    left = left_ref[...]
    strengths = twice_diagonal(strengths_ref[...])
    paired = jnp.concatenate(
        [
            jnp.concatenate(
                [remesh_ref[at : at + EDGE, :], remesh_ref[at + EDGE : at + 2 * EDGE, :]], axis=1
            )
            for at in range(0, GROUP * EDGE, 2 * EDGE)
        ],
        axis=0,
    )
    vortex = jnp.dot(paired, strengths, preferred_element_type=jnp.float32).astype(jnp.bfloat16)
    for pair in range(GROUP // 2):
        both = jnp.dot(
            left, vortex[pair * EDGE : (pair + 1) * EDGE], preferred_element_type=jnp.float32
        )
        for half in range(2):
            tile = 2 * pair + half
            for quarter in range(4):
                for side in range(2):
                    start = quarter * 32 + side * 16
                    scratch[
                        side, pl.ds(quarter * 16 * PITCH + tile, 16, stride=PITCH), :
                    ] = both[start : start + 16, half * EDGE : (half + 1) * EDGE]
    for side in range(2):
        for piece in range(64):
            out_ref[piece, :, side * EDGE : (side + 1) * EDGE] = scratch[
                side, piece * PITCH : piece * PITCH + GROUP, :
            ].astype(jnp.bfloat16)


def tile_pieces(remesh, strengths, left):
    tiles = remesh.shape[0] // EDGE
    return pl.pallas_call(
        pieces_kernel,
        grid=(tiles // GROUP,),
        in_specs=[
            pl.BlockSpec((GROUP * EDGE, EDGE), lambda g: (g, 0)),
            pl.BlockSpec((EDGE, EDGE), lambda g: (0, 0)),
            pl.BlockSpec((EDGE, EDGE), lambda g: (0, 0)),
        ],
        out_specs=pl.BlockSpec((64, GROUP, 2 * EDGE), lambda g: (0, g, 0)),
        out_shape=jax.ShapeDtypeStruct((64, tiles, 2 * EDGE), jnp.bfloat16),
        scratch_shapes=[pltpu.VMEM((2, 65 * PITCH, EDGE), jnp.float32)],
        compiler_params=pltpu.CompilerParams(vmem_limit_bytes=60 * 1024 * 1024),
    )(remesh, strengths, left)


def gather_kernel(index_ref, remesh_ref, out_ref, wide, picked):
    wide[...] = remesh_ref[...].astype(jnp.float32)

    def some(step, carry):
        for k in range(16):
            slot = step * 16 + k
            picked[pl.ds(slot, 1), :] = wide[pl.ds(index_ref[slot], 1), :]
        return carry

    lax.fori_loop(0, out_ref.shape[0] // 16, some, 0)
    out_ref[...] = picked[...].astype(jnp.bfloat16)


def gathered_rows(index, remesh):
    slots = index.shape[0]
    return pl.pallas_call(
        gather_kernel,
        in_specs=[
            pl.BlockSpec(memory_space=pltpu.SMEM),
            pl.BlockSpec(memory_space=pltpu.VMEM),
        ],
        out_specs=pl.BlockSpec(memory_space=pltpu.VMEM),
        out_shape=jax.ShapeDtypeStruct((slots, EDGE), jnp.bfloat16),
        scratch_shapes=[
            pltpu.VMEM(remesh.shape, jnp.float32),
            pltpu.VMEM((slots, EDGE), jnp.float32),
        ],
        compiler_params=pltpu.CompilerParams(vmem_limit_bytes=60 * 1024 * 1024),
        cost_estimate=pl.CostEstimate(flops=0, bytes_accessed=16 * 1024 * 1024, transcendentals=0),
    )(index, remesh)


def sums_kernel(quarter_ref, position_ref, arrived_ref, out_ref, spread):
    depth = 1024
    blocks = 64
    row = lax.broadcasted_iota(jnp.int32, (12 * blocks, EDGE), 0)
    wanted = (row % blocks) * 12 + row // blocks
    total = None
    for first in range(0, arrived_ref.shape[0], depth):
        picker = jnp.concatenate(
            [
                (wanted == position_ref[:, start : start + EDGE]).astype(jnp.bfloat16)
                for start in range(first, first + depth, EDGE)
            ],
            axis=1,
        )
        part = jnp.dot(
            picker, arrived_ref[first : first + depth, :], preferred_element_type=jnp.float32
        )
        total = part if total is None else total + part
    late = quarter_ref[0] >= 2
    block = lax.broadcasted_iota(jnp.int32, (blocks, EDGE), 0)
    for side in range(2):
        lanes = slice(side * EDGE, (side + 1) * EDGE)
        places = [total[p * blocks : (p + 1) * blocks, lanes] for p in range(12)]
        for component in range(3):
            before = pltpu.roll(places[component * 4 + 3], 1, 0)
            after = pltpu.roll(places[component * 4], blocks - 1, 0)
            places.append(
                jnp.where(
                    late,
                    jnp.where(block > 0, before, 0.0),
                    jnp.where(block < blocks - 1, after, 0.0),
                )
            )
        places.append(jnp.zeros((blocks, EDGE), jnp.float32))
        for entry, value in enumerate(places):
            spread[side, pl.ds(entry, blocks, stride=ROW_PITCH), :] = value
        for k in range(blocks):
            out_ref[16 * k : 16 * k + 16, lanes] = spread[
                side, ROW_PITCH * k : ROW_PITCH * k + 16, :
            ].astype(jnp.bfloat16)


def tile_sums(quarter, position, arrived):
    vmem = pl.BlockSpec(memory_space=pltpu.VMEM)
    return pl.pallas_call(
        sums_kernel,
        in_specs=[pl.BlockSpec(memory_space=pltpu.SMEM), vmem, vmem],
        out_specs=vmem,
        out_shape=jax.ShapeDtypeStruct((1024, 2 * EDGE), jnp.bfloat16),
        scratch_shapes=[pltpu.VMEM((2, 65 * ROW_PITCH, EDGE), jnp.float32)],
        compiler_params=pltpu.CompilerParams(vmem_limit_bytes=16 * 1024 * 1024),
    )(quarter, position, arrived)


def widen(out_ref, centre, low, high):
    edge = jnp.zeros((1, EDGE), jnp.float32)
    out_ref[0:FRONT, :] = jnp.concatenate([edge, low], axis=0)
    out_ref[FRONT + SPAN : WIDE, :] = jnp.concatenate([high, edge], axis=0)
    out_ref[FRONT : FRONT + SPAN, :] = centre


def field_of(velocity_ref, stretch_ref, coupling_ref, f):
    if f < 3:
        return velocity_ref.at[f]
    return stretch_ref.at[f - 3] if f < 6 else coupling_ref


def slabs_kernel(
    velocity_ref, stretch_ref, coupling_ref, low_ref, high_ref, last_ref, first_ref, held
):
    blank = jnp.zeros((SLAB - WIDE, EDGE), jnp.float32)
    for f in range(7):
        field = field_of(velocity_ref, stretch_ref, coupling_ref, f)
        depth = 3 if f < 3 else 2
        at = 3 * f if f < 3 else 9 + 2 * (f - 3)
        for k in range(depth):
            for out_ref, layer in ((last_ref, 16 - depth + k), (first_ref, k)):
                one = held.at[0 if out_ref is last_ref else 1, at + k]
                widen(one, field[layer], low_ref[f, layer], high_ref[f, layer])
                out_ref[at + k] = jnp.concatenate([one[...], blank], axis=0).astype(jnp.bfloat16)


def slabs(velocity, stretch, coupling, low, high):
    vmem = pl.BlockSpec(memory_space=pltpu.VMEM)
    return pl.pallas_call(
        slabs_kernel,
        in_specs=[vmem] * 5,
        out_specs=[vmem] * 2,
        out_shape=[jax.ShapeDtypeStruct((17, SLAB, EDGE), jnp.bfloat16)] * 2,
        scratch_shapes=[pltpu.VMEM((2, 17, WIDE, EDGE), jnp.float32)],
        compiler_params=pltpu.CompilerParams(vmem_limit_bytes=16 * 1024 * 1024),
    )(velocity, stretch, coupling, low, high)


def unforced(source, at, squares, halves, keep, lanes):
    centre = [source[c, at] for c in range(3)]
    carried = [h * u for h, u in zip(halves, centre)]
    ahead_weight = [s - a for s, a in zip(squares, carried)]
    behind_weight = [s + a for s, a in zip(squares, carried)]
    ahead_weight[2] = jnp.where(lanes < EDGE - 1, ahead_weight[2], 0.0)
    behind_weight[2] = jnp.where(lanes > 0, behind_weight[2], 0.0)
    results = []
    for c in range(3):
        total = keep * centre[c]
        total = total + ahead_weight[0] * source[c, at + 1]
        total = total + behind_weight[0] * source[c, at - 1]
        total = total + ahead_weight[1] * pltpu.roll(centre[c], WIDE - 1, 0)
        total = total + behind_weight[1] * pltpu.roll(centre[c], 1, 0)
        total = total + ahead_weight[2] * pltpu.roll(centre[c], EDGE - 1, 1)
        total = total + behind_weight[2] * pltpu.roll(centre[c], 1, 1)
        results.append(total)
    return results


def entry_of(component, layer):
    chord = layer - 2
    entry = component * 4 + chord // 4 if 0 <= chord < 16 else 12 + component
    return chord % 4, entry


def slab_layer(ref, k):
    return ref[k].astype(jnp.float32)[:WIDE]


def front_kernel(
    sums_ref,
    right_ref,
    velocity_ref,
    stretch_ref,
    coupling_ref,
    span_low,
    span_high,
    low_ref,
    high_ref,
    target_ref,
    base_ref,
    squares_ref,
    halves_ref,
    keep_ref,
    rate_ref,
    velocity,
    metric,
    spread,
):
    blank = jnp.zeros((8, EDGE), jnp.float32)
    lanes = lax.broadcasted_iota(jnp.int32, (WIDE, EDGE), 1)
    product = jnp.dot(
        sums_ref[...], twice_diagonal(right_ref[...]), preferred_element_type=jnp.float32
    )
    for side in range(2):
        for piece in range(64):
            spread[side, piece * ROW_PITCH : piece * ROW_PITCH + 16, :] = product[
                piece * 16 : piece * 16 + 16, side * EDGE : (side + 1) * EDGE
            ]

    for c in range(3):
        for k in range(3):
            velocity[c, k] = slab_layer(low_ref, 3 * c + k)
            velocity[c, 19 + k] = slab_layer(high_ref, 3 * c + k)
    for f in range(7):
        field = field_of(velocity_ref, stretch_ref, coupling_ref, f)
        for layer in range(16):
            widen(
                velocity.at[f, layer + 3] if f < 3 else metric.at[f - 3, layer],
                field[layer],
                span_low[f, layer],
                span_high[f, layer],
            )

    for layer in range(20):
        inner = layer - 2
        if 0 <= inner < 16:
            stretch = [metric[d, inner] for d in range(3)]
            rate = metric[3, inner]
        else:
            slab, k = (low_ref, layer) if inner < 0 else (high_ref, inner - 16)
            stretch = [slab_layer(slab, 9 + 2 * d + k) for d in range(3)]
            rate = slab_layer(slab, 15 + k)
        squares = [(step_size * viscosity) * s * s for s in stretch]
        halves = [(0.5 * step_size) * s for s in stretch]
        keep = 1.0 - rate - 2.0 * (squares[0] + squares[1] + squares[2])
        results = unforced(velocity, layer + 1, squares, halves, keep, lanes)
        for d in range(3):
            squares_ref[d, layer] = squares[d]
            halves_ref[d, layer] = halves[d]
            base_ref[d, layer] = results[d]
        keep_ref[layer] = keep
        rate_ref[layer] = rate
        for component in range(3):
            quarter, entry = entry_of(component, layer)
            target_ref[component, layer, 0:FRONT, :] = blank[:FRONT]
            target_ref[component, layer, FRONT + SPAN : WIDE, :] = blank[:FRONT]
            for side in range(2):
                start = FRONT + 16 * side
                target_ref[component, layer, start : start + 16, :] = spread[
                    side, pl.ds(quarter * 16 * ROW_PITCH + entry, 16, stride=ROW_PITCH), :
                ]


def fronted(sums, right, fields, low, high):
    vmem = pl.BlockSpec(memory_space=pltpu.VMEM)
    return pl.pallas_call(
        front_kernel,
        in_specs=[vmem] * 9,
        out_specs=[vmem] * 6,
        out_shape=[jax.ShapeDtypeStruct((3, 20, WIDE, EDGE), jnp.float32)] * 4
        + [jax.ShapeDtypeStruct((20, WIDE, EDGE), jnp.float32)] * 2,
        scratch_shapes=[
            pltpu.VMEM((3, 22, WIDE, EDGE), jnp.float32),
            pltpu.VMEM((4, 16, WIDE, EDGE), jnp.float32),
            pltpu.VMEM((2, 65 * ROW_PITCH, EDGE), jnp.float32),
        ],
        compiler_params=pltpu.CompilerParams(vmem_limit_bytes=16 * 1024 * 1024),
        cost_estimate=pl.CostEstimate(
            flops=164 * 1000 * 1000, bytes_accessed=8 * 1024 * 1024, transcendentals=0
        ),
    )(sums, right, *fields, low, high)


def grid_kernel(
    target_ref,
    low_ref,
    high_ref,
    right_ref,
    base_ref,
    squares_ref,
    halves_ref,
    keep_ref,
    rate_ref,
    slot_ref,
    next_ref,
    out_ref,
    side_sums,
    forced,
    first,
    second,
    rows,
    slots,
    done,
    sems,
):
    right = right_ref[...]
    back = FRONT + SPAN
    lanes = lax.broadcasted_iota(jnp.int32, (WIDE, EDGE), 1)
    for side, ref in enumerate((low_ref, high_ref)):
        side_sums[side, 0:128, :] = jnp.dot(ref[...], right, preferred_element_type=jnp.float32)
    slots[...] = jnp.zeros_like(slots)
    for c in range(3):
        for layer in range(20):
            quarter, entry = entry_of(c, layer)
            forced[c, layer] = target_ref[c, layer]
            forced[c, layer, FRONT - 2 : FRONT, :] = side_sums[
                0, pl.ds(quarter * 32 + entry, 2, stride=16), :
            ]
            forced[c, layer, back : back + 2, :] = side_sums[
                1, pl.ds(quarter * 32 + entry, 2, stride=16), :
            ]
    for layer in range(20):
        rate = rate_ref[layer]
        for c in range(3):
            pull = rate * forced[c, layer]
            forced[c, layer] = pull
            first[c, layer] = base_ref[c, layer] + pull

    def second_step(layer):
        results = unforced(
            first,
            layer + 1,
            [squares_ref[d, layer + 1] for d in range(3)],
            [halves_ref[d, layer + 1] for d in range(3)],
            keep_ref[layer + 1],
            lanes,
        )
        for c in range(3):
            second[c, layer] = results[c] + forced[c, layer + 1]

    def curl(layer):
        whole = [second[c, layer + 1] for c in range(3)]
        half = [halves_ref[d, layer + 2] for d in range(3)]

        def slope(d, c):
            if d == 0:
                return half[0] * (second[c, layer + 2] - second[c, layer])
            if d == 1:
                ahead = pltpu.roll(whole[c], WIDE - 1, 0)
                behind = pltpu.roll(whole[c], 1, 0)
            else:
                ahead = jnp.where(lanes < EDGE - 1, pltpu.roll(whole[c], EDGE - 1, 1), 0.0)
                behind = jnp.where(lanes > 0, pltpu.roll(whole[c], 1, 1), 0.0)
            return half[d] * (ahead - behind)

        parts = (
            slope(1, 2) - slope(2, 1),
            slope(2, 0) - slope(0, 2),
            slope(0, 1) - slope(1, 0),
        )
        for c in range(3):
            start = (c * 16 + layer) * SPAN
            rows[start : start + SPAN, :] = (1.0 / step_size) * parts[c][FRONT:back]
            done[c, layer] = whole[c][FRONT:back]

    def scatter(layer):
        for c in range(3):
            start = (c * 16 + layer) * SPAN
            for row in range(start, start + SPAN):
                slots[pl.ds(slot_ref[row], 1), :] = rows[row : row + 1, :]

    copies = []
    for layer in range(18):
        second_step(layer)
        if layer >= 2:
            curl(layer - 2)
            scatter(layer - 2)
        if layer in (9, 17):
            part = len(copies)
            copies.append(
                pltpu.make_async_copy(
                    done.at[:, pl.ds(8 * part, 8)], next_ref.at[:, pl.ds(8 * part, 8)], sems.at[part]
                )
            )
            copies[part].start()
    out_ref[...] = slots[...].astype(jnp.bfloat16)
    for copy in copies:
        copy.wait()


def grid_update(target, low, high, right, base, squares, halves, keep, rate, slot):
    vmem = pl.BlockSpec(memory_space=pltpu.VMEM)
    return pl.pallas_call(
        grid_kernel,
        in_specs=[vmem] * 9 + [pl.BlockSpec(memory_space=pltpu.SMEM)],
        out_specs=[pl.BlockSpec(memory_space=pl.ANY), vmem],
        out_shape=[
            jax.ShapeDtypeStruct((3, 16, SPAN, EDGE), jnp.float32),
            jax.ShapeDtypeStruct((2 * slot.shape[0], EDGE), jnp.bfloat16),
        ],
        scratch_shapes=[
            pltpu.VMEM((2, 144, EDGE), jnp.float32),
            pltpu.VMEM((3, 20, WIDE, EDGE), jnp.float32),
            pltpu.VMEM((3, 20, WIDE, EDGE), jnp.float32),
            pltpu.VMEM((3, 18, WIDE, EDGE), jnp.float32),
            pltpu.VMEM((slot.shape[0], EDGE), jnp.float32),
            pltpu.VMEM((2 * slot.shape[0], EDGE), jnp.float32),
            pltpu.VMEM((3, 16, SPAN, EDGE), jnp.float32),
            pltpu.SemaphoreType.DMA((2,)),
        ],
        compiler_params=pltpu.CompilerParams(vmem_limit_bytes=24 * 1024 * 1024),
    )(target, low, high, right, base, squares, halves, keep, rate, slot)


def edges_kernel(sums_ref, left_ref, right_ref):
    for quarter in range(4):
        for k in range(2):
            row = 32 * quarter + 16 * k
            left_ref[row : row + 16, :] = sums_ref[16 * quarter + k, :, :EDGE]
            right_ref[row : row + 16, :] = sums_ref[16 * quarter + 14 + k, :, EDGE:]


def edges(sums):
    vmem = pl.BlockSpec(memory_space=pltpu.VMEM)
    return pl.pallas_call(
        edges_kernel,
        in_specs=[vmem],
        out_specs=[vmem] * 2,
        out_shape=[jax.ShapeDtypeStruct((128, EDGE), jnp.bfloat16)] * 2,
        compiler_params=pltpu.CompilerParams(vmem_limit_bytes=16 * 1024 * 1024),
    )(sums)


def chain(count):
    forward = [(i, i + 1) for i in range(count - 1)]
    return forward, [(target, source) for source, target in forward]


def slot_ranks(destination, block_count):
    count = destination.shape[0]
    one_hot = (destination[:, None] == jnp.arange(block_count, dtype=jnp.int32)[None, :]).astype(
        jnp.bfloat16
    )
    positions = jnp.arange(count, dtype=jnp.int32)
    lower = (positions[:, None] > positions[None, :]).astype(jnp.bfloat16)
    before = jnp.dot(lower, one_hot, preferred_element_type=jnp.float32)
    return jnp.sum(before * one_hot.astype(jnp.float32), axis=1).astype(jnp.int32)


def arrival_places(destination, places, receiver, capacity):
    count = destination.shape[1]
    to_me = destination == receiver
    positions = jnp.arange(count, dtype=jnp.int32)
    upper = (positions[:, None] < positions[None, :]).astype(jnp.bfloat16)
    rank = jnp.dot(
        to_me.astype(jnp.bfloat16), upper, preferred_element_type=jnp.float32
    ).astype(jnp.int32)
    rank = jnp.where(to_me, rank, -1)
    matches = rank[:, None, :] == jnp.arange(capacity, dtype=jnp.int32)[None, :, None]
    return jnp.sum(jnp.where(matches, places[:, None, :], 0), axis=2).reshape(-1)


def shards(
    velocity,
    stretch,
    coupling,
    strengths,
    remesh,
    green_left,
    green_right,
    tile_owner,
    tile_place,
    row_dest,
    row_place,
):
    blocks = lax.axis_size("blk")
    spans = lax.axis_size("span")
    my_block = lax.axis_index("blk")
    my_span = lax.axis_index("span")
    tile_count = remesh.shape[0] // EDGE
    grid_count = velocity.shape[0] * velocity.shape[1] * velocity.shape[2]
    row_cap = 2 * grid_count // blocks

    pieces = tile_pieces(remesh, strengths, green_left)
    held = (
        velocity,
        stretch,
        coupling,
        tile_owner,
        tile_place,
        row_dest,
        row_place,
    )
    pieces, held = lax.optimization_barrier((pieces, held))
    velocity, stretch, coupling, tile_owner, tile_place, row_dest, row_place = held
    arrived = lax.all_to_all(pieces, "blk", split_axis=0, concat_axis=0, tiled=True)

    def mine(values, count):
        rows = values.reshape(blocks, spans * count // EDGE, EDGE)
        if count >= EDGE:
            part = lax.dynamic_slice_in_dim(
                rows, my_span * (count // EDGE), count // EDGE, axis=1
            )
            return part.reshape(blocks, count)
        whole = rows.reshape(blocks, spans, count)
        return lax.dynamic_index_in_dim(whole, my_span, 1, keepdims=False)

    owners = mine(tile_owner.T, tile_count).reshape(1, -1)
    places = mine(tile_place, tile_count).reshape(1, -1)
    position = owners * 12 + places
    quarter = jnp.reshape(my_block // 16, (1,)).astype(jnp.int32)

    forward, backward = chain(spans)
    fields = (velocity, stretch, coupling[None])
    low = lax.ppermute(
        jnp.concatenate([f[:, :, -REACH:] for f in fields], axis=0), "span", forward
    )
    high = lax.ppermute(
        jnp.concatenate([f[:, :, :REACH] for f in fields], axis=0), "span", backward
    )

    last, opening = slabs(velocity, stretch, coupling, low, high)
    extended = (velocity, stretch, coupling, low, high)
    block_forward, block_backward = chain(blocks)
    low = lax.ppermute(last, "blk", block_forward)
    high = lax.ppermute(opening, "blk", block_backward)

    destinations = mine(row_dest.T, grid_count)
    row_places = mine(row_place, grid_count)
    dest_mine = lax.dynamic_index_in_dim(destinations, my_block, 0, keepdims=False)
    row_slot = dest_mine * row_cap + slot_ranks(dest_mine, blocks)
    row_where = arrival_places(destinations, row_places, my_block, row_cap)
    remesh_rows = gathered_rows(row_where, remesh)

    arrived, position, row_slot, remesh_rows = lax.optimization_barrier(
        (arrived, position, row_slot, remesh_rows)
    )
    sums = tile_sums(quarter, position, arrived.reshape(-1, 2 * EDGE))
    sums, extended, low, high = lax.optimization_barrier((sums, extended, low, high))
    sums = lax.all_to_all(
        sums.reshape(blocks, 16, 2 * EDGE), "blk", split_axis=0, concat_axis=0, tiled=True
    )
    left_edge, right_edge = edges(sums)
    target, base, squares, halves, keep, rate = fronted(
        sums.reshape(-1, 2 * EDGE), green_right, extended, low, high
    )
    low = lax.ppermute(right_edge, "span", forward)
    high = lax.ppermute(left_edge, "span", backward)
    current, outgoing = grid_update(
        target,
        low,
        high,
        green_right,
        base,
        squares,
        halves,
        keep,
        rate,
        row_slot,
    )
    incoming = lax.all_to_all(
        outgoing.reshape(blocks, row_cap, EDGE), "blk", split_axis=0, concat_axis=0, tiled=True
    )
    spread = lax.dot_general(
        remesh_rows,
        incoming.reshape(-1, EDGE),
        (((0,), (0,)), ((), ())),
        preferred_element_type=jnp.float32,
    )
    return current, (1.0 - blend) * strengths.astype(jnp.float32) + blend * spread


def solution(mesh):
    placed = (
        P(None, "blk", "span", None),
        P(None, "blk", "span", None),
        P("blk", "span", None),
        P(("blk", "span"), None),
        P(("blk", "span"), None),
        P(),
        P(),
        P(),
        P(),
        P(),
        P(),
    )
    return jax.shard_map(
        shards,
        mesh=mesh,
        in_specs=placed,
        out_specs=(P(None, "blk", "span", None), P(("blk", "span"), None)),
        check_vma=False,
    )
```
